128 devices in a mesh: fsdp: 8 (over z, core), tp: 16 (over x, y).
Axes of the slice: x: 4, y: 4, z: 4, core: 2. Of those that a mesh axis runs over, the one named last changes fastest.
Arguments:
- momentum: float32 [8192, 14336], P('fsdp', 'tp'), may hold values from -6 to 6
- gradient: bfloat16 [8192, 14336], P('fsdp', 'tp'), may hold values from -6 to 6
- basis: float32 [14336, 512], P('tp'), may hold values from -6 to 6
Outputs:
- momentum_out: float32 [8192, 14336], P('fsdp', 'tp')
- basis_out: float32 [14336, 512], P('tp')
- update: bfloat16 [8192, 14336], P('fsdp', 'tp')
The draws below stay inside these ranges and needn't reach their ends.
All inputs are finite; a program needn't handle non-finite values.
Results may differ from the reference program's by a relative error of at most 0.0015.
Values sent between devices are 32-bit elements; how exact they have to be, the bound alone decides.
A program may use at most 64 MiB of HBM per device.

```python
import jax
import jax.numpy as jnp
from jax import lax

ROWS = 8192
COLS = 14336
RANK = 512


def steps_of(stream_key, dims, pieces, least, high):
    def one(dim, blocks):
        steps = jax.random.uniform(jax.random.fold_in(jax.random.fold_in(stream_key, 6), dim), (blocks,), jnp.float32, least / len(pieces), high / len(pieces))
        return jnp.repeat(jnp.exp(steps), dims[dim] // blocks).reshape((-1,) + (1,) * (len(dims) - dim - 1))

    loudness = one(*pieces[0])
    for cut in pieces[1:]:
        loudness = loudness * one(*cut)
    return loudness


def centred(key, dims, deviation, bound, shards=(), kind=jnp.bfloat16):
    loudness = steps_of(key, dims, shards, -0.22, 0.18) if shards else 1.0
    drawn = jax.random.normal(key, dims, jnp.float32) * deviation * loudness
    return jnp.minimum(jnp.maximum(drawn, -bound), bound).astype(kind)


def setup_inputs(seed: int = 0) -> dict:
    key_of = jax.random.split(jax.random.key(seed), 4)
    return {
        "momentum": centred(key_of[0], (ROWS, COLS), 1.0, 6.0, ((0, 8), (1, 16)), jnp.float32),
        "gradient": centred(key_of[1], (ROWS, COLS), 1.0, 6.0, ((0, 8), (1, 16))),
        "basis": centred(key_of[2], (COLS, RANK), 1.0, 6.0, ((0, 16),), jnp.float32),
    }


def reference(momentum, gradient, basis):
    high = lax.Precision.HIGHEST
    buffer = momentum + gradient.astype(jnp.float32)
    proj = jnp.dot(buffer, basis, precision=high) / jnp.sqrt(jnp.float32(COLS))
    gram = jnp.dot(proj.T, proj, precision=high)
    shift = 0.0001 * jnp.trace(gram) / RANK
    lower = jnp.linalg.cholesky(gram + shift * jnp.eye(RANK, dtype=jnp.float32))
    ortho = lax.linalg.triangular_solve(lower, proj, left_side=False, lower=True, transpose_a=True)
    back = jnp.dot(buffer.T, ortho, precision=high)
    momentum_out = buffer - 0.05 * jnp.dot(ortho, back.T, precision=high)
    scales = jnp.sqrt(lax.optimization_barrier(jnp.sum(back * back, axis=0)) / COLS + 1e-06)
    basis_out = back / scales
    update = (jnp.sqrt(jnp.float32(ROWS) / RANK) * jnp.dot(ortho, basis_out.T, precision=high)).astype(jnp.bfloat16)
    return (momentum_out, basis_out, update)
```

```python
import jax, jax.numpy as jnp
from jax import lax
from jax.experimental import pallas as pl
from jax.experimental.pallas import tpu as pltpu
from jax.sharding import PartitionSpec as P

def lane(v, j, mode):
    if mode == 0:
        return jnp.broadcast_to(v[:, j:j+1], v.shape)
    return jnp.take_along_axis(v, jnp.full(v.shape, j, jnp.int32), axis=1)

def sub(v, j, mode):
    if mode == 0:
        return jnp.broadcast_to(v[j:j+1, :], v.shape)
    return jnp.take_along_axis(v, jnp.full(v.shape, j, jnp.int32), axis=0)

def chol_inv_128(g, mode=0, n=16):
    sid = lax.broadcasted_iota(jnp.int32, (8, 128), 0)
    lid = lax.broadcasted_iota(jnp.int32, (8, 128), 1)
    x = [jnp.where(lid == sid + 8 * s, 1.0, 0.0).astype(jnp.float32) for s in range(n)]
    out = []
    for s in range(n):
        P, Q = g[s], x[s]
        look = s + 1 < n
        cb = [lane(P, 8 * s + j, mode) for j in range(8)]
        if look:
            N, NX = g[s + 1], x[s + 1]
            cn = [lane(N, 8 * s + j, mode) for j in range(8)]
        for j in range(8):
            d = 1.0 / sub(cb[j], j, mode)
            cm = jnp.where(sid > j, cb[j], 0.0)
            for k in range(j + 1, 8):
                m = sub(cb[k], j, mode) * d
                cb[k] = cb[k] - cm * m
                if look:
                    cn[k] = cn[k] - cn[j] * m
            u, ux = sub(P, j, mode) * d, sub(Q, j, mode) * d
            P, Q = P - cm * u, Q - cm * ux
            if look:
                N, NX = N - cn[j] * u, NX - cn[j] * ux
        pv = cb[0]
        for j in range(1, 8):
            pv = jnp.where(sid == j, cb[j], pv)
        r = lax.rsqrt(pv)
        R, RX = P * r, Q * r
        out.append(RX)
        if look:
            g[s + 1], x[s + 1] = N, NX
        if s + 2 < n:
            T = R.T
            rb = [sub(R, j, mode) for j in range(8)]
            rxb = [sub(RX, j, mode) for j in range(8)]
            for i in range(s + 2, n):
                Ti = T[8 * i:8 * i + 8, :]
                gi, xi = g[i], x[i]
                for j in range(8):
                    l = jnp.broadcast_to(Ti[:, j:j+1], (8, 128))
                    gi = gi - l * rb[j]
                    xi = xi - l * rxb[j]
                g[i], x[i] = gi, xi
    return out

HI = lax.Precision.HIGHEST

def chol_kernel(mode, g_ref, x_ref, s_ref, d_ref):
    n = g_ref.shape[0]
    nb = n // 128
    rid = lax.broadcasted_iota(jnp.int32, (n, n), 0)
    cid = lax.broadcasted_iota(jnp.int32, (n, n), 1)
    G = g_ref[...]
    eye = jnp.where(rid == cid, 1.0, 0.0)
    shift = jnp.sum(G * eye) * (0.0001 / n)
    s_ref[...] = G + shift * eye

    def step(k, c):
        o = pl.multiple_of(k * 128, 128)
        tiles = [s_ref[pl.ds(o + 8 * i, 8), pl.ds(o, 128)] for i in range(16)]
        out = chol_inv_128(tiles, mode)
        for i in range(16):
            d_ref[8 * i:8 * i + 8, :] = out[i]
        e128 = jnp.where(lax.broadcasted_iota(jnp.int32, (128, 128), 0) == lax.broadcasted_iota(jnp.int32, (128, 128), 1), 1.0, 0.0).astype(jnp.float32)
        s_ref[pl.ds(o, 128), pl.ds(o, 128)] = e128
        R = jnp.dot(d_ref[...], s_ref[pl.ds(o, 128), :], precision=HI, preferred_element_type=jnp.float32)
        s_ref[pl.ds(o, 128), :] = R
        def row(i, c):
            oi = pl.multiple_of(i * 128, 128)
            L = s_ref[pl.ds(o, 128), pl.ds(oi, 128)]
            s_ref[pl.ds(oi, 128), pl.ds(o, 128)] = jnp.zeros((128, 128), jnp.float32)
            s_ref[pl.ds(oi, 128), :] -= lax.dot_general(L, s_ref[pl.ds(o, 128), :], (((0,), (0,)), ((), ())), precision=HI, preferred_element_type=jnp.float32)
            return c
        lax.fori_loop(k + 1, nb, row, 0)
        return c
    lax.fori_loop(0, nb, step, 0)
    x_ref[...] = jnp.where(cid <= rid, s_ref[...], 0.0)

def chol_inv(G, mode=0, **kw):
    n = G.shape[0]
    return pl.pallas_call(
        lambda *a: chol_kernel(mode, *a),
        out_shape=jax.ShapeDtypeStruct((n, n), jnp.float32),
        scratch_shapes=[pltpu.VMEM((n, n), jnp.float32), pltpu.VMEM((128, 128), jnp.float32)],
        compiler_params=pltpu.CompilerParams(vmem_limit_bytes=50 * 2**20), **kw)(G)

ROWS = 8192
COLS = 14336
RANK = 512


def shards(momentum, gradient, basis):
    high = lax.Precision.HIGHEST
    buffer = momentum + gradient.astype(jnp.float32)
    inv_cols = 1.0 / jnp.sqrt(jnp.float32(COLS))
    partial_proj = jnp.dot(buffer, basis, precision=high) * inv_cols
    proj = lax.psum(partial_proj, "tp")
    gram = lax.psum(jnp.dot(proj.T, proj, precision=high), "fsdp")
    inverse = chol_inv(gram, 1)
    ortho = jnp.dot(proj, inverse.T, precision=high)
    partial_back = lax.dot_general(buffer, ortho, (((0,), (0,)), ((), ())), precision=high)
    back = lax.psum(partial_back, "fsdp")
    sums = lax.psum(jnp.sum(back * back, axis=0), "tp")
    momentum_out = buffer - 0.05 * jnp.dot(ortho, back.T, precision=high)
    scales = jnp.sqrt(sums / COLS + 1e-06)
    basis_out = back / scales
    update = (
        jnp.sqrt(jnp.float32(ROWS) / RANK) * jnp.dot(ortho, basis_out.T, precision=high)
    ).astype(jnp.bfloat16)
    return (momentum_out, basis_out, update)


def solution(mesh):
    placed = (P("fsdp", "tp"), P("fsdp", "tp"), P("tp", None))
    return jax.shard_map(
        shards,
        mesh=mesh,
        in_specs=placed,
        out_specs=(P("fsdp", "tp"), P("tp", None), P("fsdp", "tp")),
        check_vma=False,
    )
```

```python
import functools

import jax
import jax.numpy as jnp
from jax import lax
from jax.experimental import pallas as pl
from jax.experimental.pallas import tpu as pltpu
from jax.sharding import PartitionSpec as P

ROWS = 8192
COLS = 14336
RANK = 512
HI = lax.Precision.HIGHEST
F32 = jnp.float32
BF16 = jnp.bfloat16
MESH = pl.DeviceIdType.MESH
NT = (((1,), (1,)), ((), ()))
TN = (((0,), (0,)), ((), ()))
NN = (((1,), (0,)), ((), ()))


def split(v):
    high = v.astype(BF16)
    return high, (v - high.astype(F32)).astype(BF16)


def dot3(ah, al, bh, bl, dims=NN):
    def one(a, b):
        return lax.dot_general(a, b, dims, preferred_element_type=F32)

    return one(ah, bl) + one(al, bh) + one(ah, bh)


class Links:
    def __init__(self, send_sem, recv_sem):
        self.send_sem, self.recv_sem, self.used, self.sent = send_sem, recv_sem, 0, []

    def slot(self):
        self.used += 1
        return self.used - 1

    def copy(self, slot, src, dst, device):
        return pltpu.make_async_remote_copy(
            src_ref=src,
            dst_ref=dst,
            send_sem=self.send_sem.at[slot],
            recv_sem=self.recv_sem.at[slot],
            device_id=device,
            device_id_type=MESH,
        )

    def send(self, slot, src, dst, device):
        c = self.copy(slot, src, dst, device)
        c.start()
        self.sent.append(c)

    def landed(self, slot, dst, device):
        self.copy(slot, dst, dst, device).wait_recv()

    def drain(self):
        for c in self.sent:
            c.wait_send()


class Ring:
    def __init__(self, me, at):
        self.me = me
        self.r, self.l, self.o = lax.rem(me + 1, 4), lax.rem(me + 3, 4), lax.rem(me + 2, 4)
        self.right, self.left, self.far = at(self.r), at(self.l), at(self.o)


class Reduce:
    def __init__(self, links, ring, ref, base, rows, land):
        self.k, self.g, self.ref, self.base, self.rows, self.land = links, ring, ref, base, rows, land
        self.s = [links.slot() for _ in range(6)]

    def half(self, chunk, h):
        n = self.rows // 2
        return self.ref.at[pl.ds(pl.multiple_of(self.base + chunk * self.rows + h * n, n), n), :]

    def relay(self):
        self.k.send(self.s[0], self.half(self.g.o, 0), self.land.at[0], self.g.right)
        self.k.send(self.s[1], self.half(self.g.o, 1), self.land.at[1], self.g.left)

    def direct(self):
        self.k.send(self.s[2], self.half(self.g.r, 1), self.land.at[2], self.g.right)
        self.k.send(self.s[3], self.half(self.g.l, 0), self.land.at[3], self.g.left)

    def mid(self):
        for d, (chunk, device) in enumerate(((self.g.r, self.g.right), (self.g.l, self.g.left))):
            self.k.landed(self.s[d], self.land.at[d], device)
            part = self.half(chunk, d)
            part[...] += self.land[d]
            self.k.send(self.s[4 + d], part, self.land.at[4 + d], device)

    def finish(self):
        for d in range(2, 6):
            self.k.landed(self.s[d], self.land.at[d], self.g.right)
        first = self.half(self.g.me, 0)[...] + self.land[4] + self.land[3]
        second = self.half(self.g.me, 1)[...] + self.land[5] + self.land[2]
        return first, second


class Gather:
    def __init__(self, links, ring, ref, base, rows):
        self.k, self.g, self.ref, self.base, self.rows = links, ring, ref, base, rows
        self.s = [links.slot() for _ in range(4)]

    def chunk(self, i):
        return self.ref.at[pl.ds(pl.multiple_of(self.base + i * self.rows, self.rows), self.rows), :]

    def half(self, i, h):
        n = self.rows // 2
        return self.ref.at[pl.ds(pl.multiple_of(self.base + i * self.rows + h * n, n), n), :]

    def start(self):
        own = self.chunk(self.g.me)
        self.k.send(self.s[0], own, own, self.g.right)
        self.k.send(self.s[1], own, own, self.g.left)

    def mid(self):
        self.k.landed(self.s[0], self.chunk(self.g.l), self.g.right)
        part = self.half(self.g.l, 0)
        self.k.send(self.s[2], part, part, self.g.right)
        self.k.landed(self.s[1], self.chunk(self.g.r), self.g.left)
        part = self.half(self.g.r, 1)
        self.k.send(self.s[3], part, part, self.g.left)

    def finish(self):
        self.k.landed(self.s[2], self.half(self.g.o, 0), self.g.right)
        self.k.landed(self.s[3], self.half(self.g.o, 1), self.g.left)


class SumOver8:
    def __init__(self, links, ring, core, partner, ref, pair, land, total):
        self.k, self.core, self.partner, self.ref, self.pair, self.total = links, core, partner, ref, pair, total
        self.ring = ring
        self.n = ref.shape[0] // 2
        self.s = [links.slot() for _ in range(5)]
        self.base = pl.multiple_of(core * self.n, self.n)
        self.other = pl.multiple_of((1 - core) * self.n, self.n)
        self.reduce = Reduce(links, ring, ref, self.base, self.n // 4, land)
        self.gather = Gather(links, ring, total, self.base, self.n // 4)

    def exchange(self):
        self.k.send(self.s[0], self.ref.at[pl.ds(self.other, self.n), :], self.pair, self.partner)

    def begin(self):
        self.k.landed(self.s[0], self.pair, self.partner)
        self.ref[pl.ds(self.base, self.n), :] += self.pair[...]
        self.reduce.relay()
        self.reduce.direct()

    def mid(self):
        self.reduce.mid()

    def pass_on(self, j, chunk):
        part = self.gather.chunk(chunk)
        self.k.send(self.s[1 + j], part, part, self.partner)

    def turn(self):
        first, second = self.reduce.finish()
        self.gather.half(self.ring.me, 0)[...] = first
        self.gather.half(self.ring.me, 1)[...] = second
        self.gather.start()
        self.pass_on(0, self.ring.me)

    def forward(self):
        self.gather.mid()
        self.pass_on(1, self.ring.l)
        self.pass_on(2, self.ring.r)

    def last(self):
        self.gather.finish()
        self.pass_on(3, self.ring.o)

    def end(self):
        rows = self.n // 4
        for j, chunk in enumerate((self.ring.me, self.ring.l, self.ring.r, self.ring.o)):
            at = pl.multiple_of(self.other + chunk * rows, rows)
            self.k.landed(self.s[1 + j], self.total.at[pl.ds(at, rows), :], self.partner)


def lane(v, j):
    return jnp.take_along_axis(v, jnp.full(v.shape, j, jnp.int32), axis=1)


def row(v, j):
    return jnp.broadcast_to(v[j:j + 1, :], v.shape)


def eight(s, a_ref, r_ref, t_ref):
    sid = lax.broadcasted_iota(jnp.int32, (8, 128), 0)
    o = pl.multiple_of(8 * s, 8)
    on = pl.multiple_of(8 * s + 8, 8)
    p, q = a_ref[pl.ds(o, 8), 0:128], a_ref[pl.ds(o, 8), 128:256]
    n, nx = a_ref[pl.ds(on, 8), 0:128], a_ref[pl.ds(on, 8), 128:256]
    last = r_ref[...]
    t = t_ref[pl.ds(on, 8), :]
    for j in range(8):
        l = jnp.broadcast_to(t[:, j:j + 1], (8, 128))
        n = n - l * row(last[:, 0:128], j)
        nx = nx - l * row(last[:, 128:256], j)
    cb = [lane(p, 8 * s + j) for j in range(8)]
    cn = [lane(n, 8 * s + j) for j in range(8)]
    for j in range(8):
        d = 1.0 / row(cb[j], j)
        cm = jnp.where(sid > j, cb[j], 0.0)
        for k in range(j + 1, 8):
            m = row(cb[k], j) * d
            cb[k] = cb[k] - cm * m
            cn[k] = cn[k] - cn[j] * m
        u, ux = row(p, j) * d, row(q, j) * d
        p, q = p - cm * u, q - cm * ux
        n, nx = n - cn[j] * u, nx - cn[j] * ux
    pivots = cb[0]
    for j in range(1, 8):
        pivots = jnp.where(sid == j, cb[j], pivots)
    scale = lax.rsqrt(pivots)
    p, q = p * scale, q * scale
    rest = jnp.dot(t_ref[0:128, :], last, precision=HI, preferred_element_type=F32)
    rid = lax.broadcasted_iota(jnp.int32, (128, 256), 0)
    a_ref[0:128, :] -= jnp.where(rid >= 8 * s + 16, rest, 0.0)
    a_ref[pl.ds(o, 8), 128:256] = q
    a_ref[pl.ds(on, 8), 0:128] = n
    a_ref[pl.ds(on, 8), 128:256] = nx
    r_ref[:, 0:128] = p
    r_ref[:, 128:256] = q
    t_ref[0:128, :] = p.T


def factor_step(k, s_ref, a_ref, r_ref, t_ref, event):
    n = s_ref.shape[0]
    o = 128 * k
    i128 = lax.broadcasted_iota(jnp.int32, (128, 128), 0)
    j128 = lax.broadcasted_iota(jnp.int32, (128, 128), 1)
    unit = jnp.where(i128 == j128, 1.0, 0.0).astype(F32)
    a_ref[0:128, 0:128] = s_ref[o:o + 128, o:o + 128]
    a_ref[0:128, 128:256] = unit
    a_ref[128:136, :] = jnp.zeros((8, 256), F32)
    r_ref[...] = jnp.zeros(r_ref.shape, F32)
    t_ref[...] = jnp.zeros(t_ref.shape, F32)

    def body(s, c):
        eight(s, a_ref, r_ref, t_ref)
        return c

    lax.fori_loop(0, 8, body, 0)
    event()
    lax.fori_loop(8, 16, body, 0)
    event()
    s_ref[o:o + 128, o:o + 128] = unit
    block = jnp.dot(a_ref[0:128, 128:256], s_ref[o:o + 128, :], precision=HI, preferred_element_type=F32)
    s_ref[o:o + 128, :] = block
    if o + 128 < n:
        s_ref[o + 128:, o:o + 128] = jnp.zeros((n - o - 128, 128), F32)
        s_ref[o + 128:, :] -= lax.dot_general(
            block[:, o + 128:], block, TN, precision=HI, preferred_element_type=F32
        )


def kernel_sums(
    m_ref, g_ref, v_ref,
    obf_ref, osh_ref, osl_ref, bth_ref, btl_ref, basis_ref,
    bh, bl, vh, vl, part, proj, ph, pl_, pth, ptl,
    gram, gpair, gland, gsum, inv, w, wpair, wland, wsum,
    a_ref, r_ref, t_ref, x1, y1, y2, x2, colsum, cland,
    send_sem, recv_sem,
):
    f, t = lax.axis_index("fsdp"), lax.axis_index("tp")
    z, core = lax.div(f, 2), lax.rem(f, 2)
    x, y = lax.div(t, 4), lax.rem(t, 4)
    rx = Ring(x, lambda i: (f, i * 4 + y))
    ry = Ring(y, lambda i: (f, x * 4 + i))
    rz = Ring(z, lambda i: (i * 2 + core, t))
    partner = (f + 1 - 2 * core, t)
    links = Links(send_sem, recv_sem)

    peers = (rx.right, rx.left, rx.far, ry.right, ry.left, ry.far, rz.right, rz.left, partner)
    barrier = pltpu.get_barrier_semaphore()
    for device in peers:
        pl.semaphore_signal(barrier, inc=1, device_id=device, device_id_type=MESH)
    pl.semaphore_wait(barrier, len(peers))

    rows = m_ref.shape[0]
    rank = v_ref.shape[1]
    half, r1, r2 = rows // 2, rows // 8, rows // 32
    inv_cols = 1.0 / jnp.sqrt(jnp.float32(COLS))

    vh[...], vl[...] = split(v_ref[...])
    first_a = Reduce(links, rx, part, 0, r1, x1)
    first_b = Reduce(links, ry, part, half, r1, y1)
    for d in (2, 1, 3, 0):
        ia = pl.multiple_of(lax.rem(x + d, 4) * r1, r1)
        ib = pl.multiple_of(half + lax.rem(y + d, 4) * r1, r1)
        highs, lows = [], []
        for i in (ia, ib):
            high, low = split(m_ref[pl.ds(i, r1), :] + g_ref[pl.ds(i, r1), :].astype(F32))
            bh[pl.ds(i, r1), :] = high
            bl[pl.ds(i, r1), :] = low
            highs.append(high)
            lows.append(low)
        value = dot3(jnp.concatenate(highs), jnp.concatenate(lows), vh[...], vl[...]) * inv_cols
        part[pl.ds(ia, r1), :] = value[:r1]
        part[pl.ds(ib, r1), :] = value[r1:]
        if d == 2:
            first_a.relay()
            first_b.relay()
        if d == 3:
            first_a.direct()
            first_b.direct()
    first_a.mid()
    first_b.mid()
    base_a = pl.multiple_of(x * r1, r1)
    base_b = pl.multiple_of(half + y * r1, r1)
    second_a = Reduce(links, ry, part, base_a, r2, y2)
    second_b = Reduce(links, rx, part, base_b, r2, x2)
    for one, base, two in ((first_a, base_a, second_a), (first_b, base_b, second_b)):
        h0, h1 = one.finish()
        part[pl.ds(base, r1 // 2), :] = h0
        part[pl.ds(pl.multiple_of(base + r1 // 2, r1 // 2), r1 // 2), :] = h1
        two.relay()
        two.direct()
    second_a.mid()
    second_b.mid()
    third_a = Gather(links, ry, proj, base_a, r2)
    third_b = Gather(links, rx, proj, base_b, r2)
    for two, ring, three in ((second_a, ry, third_a), (second_b, rx, third_b)):
        h0, h1 = two.finish()
        three.half(ring.me, 0)[...] = h0
        three.half(ring.me, 1)[...] = h1
        three.start()
    third_a.mid()
    third_b.mid()
    fourth_a = Gather(links, rx, proj, 0, r1)
    fourth_b = Gather(links, ry, proj, half, r1)
    third_a.finish()
    fourth_a.start()
    third_b.finish()
    fourth_b.start()
    fourth_a.mid()
    fourth_b.mid()
    fourth_a.finish()
    fourth_b.finish()

    step = 256
    def turned(i, c):
        at = pl.multiple_of(i * step, step)
        value = proj[pl.ds(at, step), :]
        ph[pl.ds(at, step), :], pl_[pl.ds(at, step), :] = split(value)
        pth[:, pl.ds(at, step)], ptl[:, pl.ds(at, step)] = split(value.T)
        return c

    lax.fori_loop(0, rows // step, turned, 0)
    tile = 128

    def gram_rows(i, c):
        at = pl.multiple_of(i * tile, tile)
        gram[pl.ds(at, tile), :] = dot3(pth[pl.ds(at, tile), :], ptl[pl.ds(at, tile), :], ph[...], pl_[...])
        return c

    lax.fori_loop(0, rank // tile, gram_rows, 0)
    gs = SumOver8(links, rz, core, partner, gram, gpair, gland, gsum)
    ws = SumOver8(links, rz, core, partner, w, wpair, wland, wsum)
    gs.exchange()
    gs.begin()

    def w_rows(i, c):
        at = pl.multiple_of(i * tile, tile)
        w[pl.ds(at, tile), :] = dot3(pth[pl.ds(at, tile), :], ptl[pl.ds(at, tile), :], bh[...], bl[...])
        return c

    lax.fori_loop(0, rank // tile, w_rows, 0)
    ws.exchange()
    gs.mid()
    gs.turn()
    gs.forward()
    gs.last()
    gs.end()

    rid = lax.broadcasted_iota(jnp.int32, (rank, rank), 0)
    cid = lax.broadcasted_iota(jnp.int32, (rank, rank), 1)
    value = gsum[...]
    diagonal = jnp.where(rid == cid, value, 0.0)
    shift = 0.0001 * jnp.sum(diagonal) / rank
    inv[...] = value + jnp.where(rid == cid, shift, 0.0)
    events = [ws.mid, ws.turn, ws.forward, ws.last, ws.end]

    def event():
        if events:
            events.pop(0)()

    ws.begin()
    for k in range(rank // 128):
        factor_step(k, inv, a_ref, r_ref, t_ref, event)
    while events:
        event()
    xh, xl = split(jnp.where(cid <= rid, inv[...], 0.0))

    wh, wl = split(wsum[...])
    back_t = dot3(xh, xl, wh, wl)
    bth_ref[...], btl_ref[...] = split(back_t)
    back = back_t.T
    total = jnp.sum(back * back, axis=0, keepdims=True)
    basis_ref[...] = back
    for ring, at in ((rx, 0), (ry, 3)):
        colsum[at // 3] = jnp.broadcast_to(total, colsum.shape[1:])
        slots = [links.slot() for _ in range(3)]
        devices = (ring.right, ring.left, ring.far)
        for j, device in enumerate(devices):
            links.send(slots[j], colsum.at[at // 3], cland.at[at + j], device)
        if at == 0:
            ortho = dot3(ph[...], pl_[...], xh, xl, NT)
            obf_ref[...] = ortho.astype(BF16)
        for j, device in enumerate(devices):
            links.landed(slots[j], cland.at[at + j], device)
        for j in range(3):
            total = total + cland[at + j, 0:1, :]
    scales = jnp.sqrt(total / COLS + 1e-06)
    osh_ref[...], osl_ref[...] = split(ortho * (jnp.sqrt(jnp.float32(ROWS) / RANK) / scales))
    basis_ref[...] = basis_ref[...] / scales
    links.drain()


def kernel_outputs(m_ref, g_ref, o_ref, osh_ref, osl_ref, bth_ref, btl_ref, b_ref, mo_ref, bo_ref, u_ref):
    buffer = m_ref[...] + g_ref[...].astype(F32)
    low = jnp.dot(o_ref[...], bth_ref[...], preferred_element_type=F32)
    mo_ref[...] = buffer - 0.05 * low
    u_ref[...] = dot3(osh_ref[...], osl_ref[...], bth_ref[...], btl_ref[...]).astype(BF16)
    bo_ref[...] = b_ref[...]


def shards(momentum, gradient, basis):
    rows, cols = momentum.shape
    rank = basis.shape[1]
    r1, r2 = rows // 8, rows // 32

    def mem(shape, kind=F32):
        return pltpu.VMEM(shape, kind)

    def out(shape, kind=F32):
        return jax.ShapeDtypeStruct(shape, kind)

    whole = pl.BlockSpec(memory_space=pltpu.VMEM)
    n = rank // 8
    obf, osh, osl, bth, btl, basis_out = pl.pallas_call(
        kernel_sums,
        out_shape=(
            out((rows, rank), BF16), out((rows, rank), BF16), out((rows, rank), BF16),
            out((rank, cols), BF16), out((rank, cols), BF16), out((cols, rank)),
        ),
        in_specs=[whole] * 3,
        out_specs=(whole,) * 6,
        scratch_shapes=[
            mem((rows, cols), BF16), mem((rows, cols), BF16), mem((cols, rank), BF16), mem((cols, rank), BF16),
            mem((rows, rank)), mem((rows, rank)),
            mem((rows, rank), BF16), mem((rows, rank), BF16), mem((rank, rows), BF16), mem((rank, rows), BF16),
            mem((rank, rank)), mem((rank // 2, rank)), mem((6, n // 2, rank)), mem((rank, rank)), mem((rank, rank)),
            mem((rank, cols)), mem((rank // 2, cols)), mem((6, n // 2, cols)), mem((rank, cols)),
            mem((136, 256)), mem((8, 256)), mem((136, 8)),
            mem((6, r1 // 2, rank)), mem((6, r1 // 2, rank)), mem((6, r2 // 2, rank)), mem((6, r2 // 2, rank)),
            mem((2, 8, rank)), mem((6, 8, rank)),
            pltpu.SemaphoreType.DMA((76,)), pltpu.SemaphoreType.DMA((76,)),
        ],
        compiler_params=pltpu.CompilerParams(
            collective_id=0, has_side_effects=True, vmem_limit_bytes=60 * 2**20
        ),
        cost_estimate=pl.CostEstimate(flops=10 * 10**9, bytes_accessed=20 * 2**20, transcendentals=0),
    )(momentum, gradient, basis)
    tiles = 4
    tr, tc = rows // tiles, cols // tiles

    def rowed(width):
        return pl.BlockSpec((tr, width), lambda i: (i, 0))

    fixed = pl.BlockSpec((rank, cols), lambda i: (0, 0))
    cut = pl.BlockSpec((tc, rank), lambda i: (i, 0))
    return pl.pallas_call(
        kernel_outputs,
        grid=(tiles,),
        out_shape=(out((rows, cols)), out((cols, rank)), out((rows, cols), BF16)),
        in_specs=[rowed(cols), rowed(cols), rowed(rank), rowed(rank), rowed(rank), fixed, fixed, cut],
        out_specs=(rowed(cols), cut, rowed(cols)),
        compiler_params=pltpu.CompilerParams(vmem_limit_bytes=40 * 2**20),
        cost_estimate=pl.CostEstimate(flops=4 * 10**9, bytes_accessed=18 * 2**20, transcendentals=0),
    )(momentum, gradient, obf, osh, osl, bth, btl, basis_out)


def solution(mesh):
    placed = (P("fsdp", "tp"), P("fsdp", "tp"), P("tp", None))
    return jax.shard_map(
        shards,
        mesh=mesh,
        in_specs=placed,
        out_specs=(P("fsdp", "tp"), P("tp", None), P("fsdp", "tp")),
        check_vma=False,
    )
```

```python
import functools

import jax
import jax.numpy as jnp
from jax import lax
from jax.experimental import pallas as pl
from jax.experimental.pallas import tpu as pltpu
from jax.sharding import PartitionSpec as P

ROWS = 8192
COLS = 14336
RANK = 512
HI = lax.Precision.HIGHEST
F32 = jnp.float32
BF16 = jnp.bfloat16
MESH = pl.DeviceIdType.MESH
NT = (((1,), (1,)), ((), ()))
TN = (((0,), (0,)), ((), ()))
NN = (((1,), (0,)), ((), ()))


def split(v):
    high = v.astype(BF16)
    return high, (v - high.astype(F32)).astype(BF16)


def dot3(ah, al, bh, bl, dims=NN):
    def one(a, b):
        return lax.dot_general(a, b, dims, preferred_element_type=F32)

    return one(ah, bl) + one(al, bh) + one(ah, bh)


class Links:
    def __init__(self, send_sem, recv_sem):
        self.send_sem, self.recv_sem, self.used, self.sent = send_sem, recv_sem, 0, []

    def slot(self):
        self.used += 1
        return self.used - 1

    def copy(self, slot, src, dst, device):
        return pltpu.make_async_remote_copy(
            src_ref=src,
            dst_ref=dst,
            send_sem=self.send_sem.at[slot],
            recv_sem=self.recv_sem.at[slot],
            device_id=device,
            device_id_type=MESH,
        )

    def send(self, slot, src, dst, device):
        c = self.copy(slot, src, dst, device)
        c.start()
        self.sent.append(c)

    def landed(self, slot, dst, device):
        self.copy(slot, dst, dst, device).wait_recv()

    def drain(self):
        for c in self.sent:
            c.wait_send()
        self.sent = []


class Ring:
    def __init__(self, me, at):
        self.me = me
        self.others = [lax.rem(me + o, 4) for o in (2, 1, 3)]
        self.devices = [at(i) for i in self.others]
        self.sources = [lax.rem(me + o, 4) for o in (2, 3, 1)]


def cut(ref, at, n):
    return ref.at[pl.ds(pl.multiple_of(at, n), n), :]


class Reduce:
    def __init__(self, links, ring, ref, base, rows, land):
        self.k, self.g, self.ref, self.base, self.rows, self.land = links, ring, ref, base, rows, land
        self.s = [links.slot() for _ in range(3)]

    def chunk(self, i):
        return cut(self.ref, self.base + i * self.rows, self.rows)

    def send(self, j):
        self.k.send(self.s[j], self.chunk(self.g.others[j]), self.land.at[j], self.g.devices[j])

    def start(self):
        for j in range(3):
            self.send(j)

    def finish(self):
        for j in range(3):
            self.k.landed(self.s[j], self.land.at[j], self.g.devices[j])
        return (self.chunk(self.g.me)[...] + self.land[0]) + (self.land[1] + self.land[2])


class Gather:
    def __init__(self, links, ring, ref, base, rows):
        self.k, self.g, self.ref, self.base, self.rows = links, ring, ref, base, rows
        self.s = [links.slot() for _ in range(3)]

    def chunk(self, i):
        return cut(self.ref, self.base + i * self.rows, self.rows)

    def start(self):
        own = self.chunk(self.g.me)
        for j in range(3):
            self.k.send(self.s[j], own, own, self.g.devices[j])

    def finish(self):
        for j in range(3):
            self.k.landed(self.s[j], self.chunk(self.g.sources[j]), self.g.devices[j])


class SumOver8:
    def __init__(self, links, ring, core, partner, ref, pair, land, total):
        self.k, self.core, self.partner, self.ref, self.pair, self.total = links, core, partner, ref, pair, total
        self.ring = ring
        self.n = ref.shape[0] // 2
        self.rows = self.n // 4
        self.s = [links.slot() for _ in range(5)]
        self.base = core * self.n
        self.other = (1 - core) * self.n
        self.reduce = Reduce(links, ring, ref, self.base, self.rows, land)
        self.gather = Gather(links, ring, total, self.base, self.rows)

    def exchange(self):
        self.k.send(self.s[0], cut(self.ref, self.other, self.n), self.pair, self.partner)

    def begin(self):
        self.k.landed(self.s[0], self.pair, self.partner)
        own = cut(self.ref, self.base, self.n)
        own[...] += self.pair[...]
        self.reduce.start()

    def pass_on(self, j, chunk):
        part = self.gather.chunk(chunk)
        self.k.send(self.s[1 + j], part, part, self.partner)

    def turn(self):
        self.gather.chunk(self.ring.me)[...] = self.reduce.finish()
        self.gather.start()
        self.pass_on(0, self.ring.me)

    def forward(self):
        self.gather.finish()
        for j in range(3):
            self.pass_on(1 + j, self.ring.sources[j])

    def end(self):
        for j, chunk in enumerate([self.ring.me] + self.ring.sources):
            self.k.landed(self.s[1 + j], cut(self.total, self.other + chunk * self.rows, self.rows), self.partner)


def lane(v, j):
    return jnp.take_along_axis(v, jnp.full(v.shape, j, jnp.int32), axis=1)


def row(v, j):
    return jnp.broadcast_to(v[j:j + 1, :], v.shape)


def eight(s, a_ref, r_ref, t_ref):
    sid = lax.broadcasted_iota(jnp.int32, (8, 128), 0)
    o = pl.multiple_of(8 * s, 8)
    on = pl.multiple_of(8 * s + 8, 8)
    p, q = a_ref[pl.ds(o, 8), 0:128], a_ref[pl.ds(o, 8), 128:256]
    n, nx = a_ref[pl.ds(on, 8), 0:128], a_ref[pl.ds(on, 8), 128:256]
    last = r_ref[...]
    t = t_ref[pl.ds(on, 8), :]
    for j in range(8):
        l = jnp.broadcast_to(t[:, j:j + 1], (8, 128))
        n = n - l * row(last[:, 0:128], j)
        nx = nx - l * row(last[:, 128:256], j)
    cb = [lane(p, 8 * s + j) for j in range(8)]
    cn = [lane(n, 8 * s + j) for j in range(8)]
    for j in range(8):
        d = 1.0 / row(cb[j], j)
        cm = jnp.where(sid > j, cb[j], 0.0)
        for k in range(j + 1, 8):
            m = row(cb[k], j) * d
            cb[k] = cb[k] - cm * m
            cn[k] = cn[k] - cn[j] * m
        u, ux = row(p, j) * d, row(q, j) * d
        p, q = p - cm * u, q - cm * ux
        n, nx = n - cn[j] * u, nx - cn[j] * ux
    pivots = cb[0]
    for j in range(1, 8):
        pivots = jnp.where(sid == j, cb[j], pivots)
    scale = lax.rsqrt(pivots)
    p, q = p * scale, q * scale
    rest = jnp.dot(t_ref[0:128, :], last, precision=HI, preferred_element_type=F32)
    rid = lax.broadcasted_iota(jnp.int32, (128, 256), 0)
    a_ref[0:128, :] -= jnp.where(rid >= 8 * s + 16, rest, 0.0)
    a_ref[pl.ds(o, 8), 128:256] = q
    a_ref[pl.ds(on, 8), 0:128] = n
    a_ref[pl.ds(on, 8), 128:256] = nx
    r_ref[:, 0:128] = p
    r_ref[:, 128:256] = q
    t_ref[0:128, :] = p.T


def factor_step(k, s_ref, a_ref, r_ref, t_ref, event):
    n = s_ref.shape[0]
    o = 128 * k
    i128 = lax.broadcasted_iota(jnp.int32, (128, 128), 0)
    j128 = lax.broadcasted_iota(jnp.int32, (128, 128), 1)
    unit = jnp.where(i128 == j128, 1.0, 0.0).astype(F32)
    a_ref[0:128, 0:128] = s_ref[o:o + 128, o:o + 128]
    a_ref[0:128, 128:256] = unit
    a_ref[128:136, :] = jnp.zeros((8, 256), F32)
    r_ref[...] = jnp.zeros(r_ref.shape, F32)
    t_ref[...] = jnp.zeros(t_ref.shape, F32)

    def body(s, c):
        eight(s, a_ref, r_ref, t_ref)
        return c

    for quarter in range(4):
        lax.fori_loop(4 * quarter, 4 * quarter + 4, body, 0)
        event()
    s_ref[o:o + 128, o:o + 128] = unit
    block = jnp.dot(a_ref[0:128, 128:256], s_ref[o:o + 128, :], precision=HI, preferred_element_type=F32)
    s_ref[o:o + 128, :] = block
    if o + 128 < n:
        s_ref[o + 128:, o:o + 128] = jnp.zeros((n - o - 128, 128), F32)
        s_ref[o + 128:, :] -= lax.dot_general(
            block[:, o + 128:], block, TN, precision=HI, preferred_element_type=F32
        )


def full(a, b, dims=NN):
    return lax.dot_general(a, b, dims, precision=HI, preferred_element_type=F32)


def kernel_sums(
    m_hbm, g_hbm, v_hbm,
    oh_hbm, ol_hbm, bth_hbm, btl_hbm, basis_hbm, sc_hbm,
    m_ref, g_ref, v_ref, oh_ref, ol_ref, bth_ref, btl_ref, basis_ref, sc_ref,
    bh, bl, vh, vl, part, proj, ph, pl_, pth, ptl,
    gram0, gpair0, gland0, gsum0, gram1, gpair1, gland1, gsum1, w, wpair, wland, wsum,
    s0, s1, s2, a_ref, r_ref, t_ref, x1, y1, y2, x2, tbuf, tland, colsum, cland,
    in_sem, out_sem, send_sem, recv_sem,
):
    f, t = lax.axis_index("fsdp"), lax.axis_index("tp")
    z, core = lax.div(f, 2), lax.rem(f, 2)
    x, y = lax.div(t, 4), lax.rem(t, 4)
    rows = m_ref.shape[0]
    rank = v_ref.shape[1]
    half, r1, r2 = rows // 2, rows // 8, rows // 32
    wide = rank // 2

    v_in = pltpu.make_async_copy(v_hbm, v_ref, in_sem.at[0])
    v_in.start()
    spans, arrivals = [], []
    for j, d in enumerate((2, 1, 3, 0)):
        pair = (
            pl.multiple_of(lax.rem(x + d, 4) * r1, r1),
            pl.multiple_of(half + lax.rem(y + d, 4) * r1, r1),
        )
        spans.append(pair)
        arrivals.append([])
        for i, at in enumerate(pair):
            for l, (src, dst) in enumerate(((m_hbm, m_ref), (g_hbm, g_ref))):
                c = pltpu.make_async_copy(
                    src.at[pl.ds(at, r1), :], dst.at[pl.ds(at, r1), :], in_sem.at[1 + 4 * j + 2 * i + l]
                )
                c.start()
                arrivals[-1].append(c)

    rx = Ring(x, lambda i: (f, i * 4 + y))
    ry = Ring(y, lambda i: (f, x * 4 + i))
    rz = Ring(z, lambda i: (i * 2 + core, t))
    partner = (f + 1 - 2 * core, t)
    plane = [(f, lax.rem(t + o, 16)) for o in range(1, 16)]
    links = Links(send_sem, recv_sem)
    peers = plane + rz.devices + [partner]
    barrier = pltpu.get_barrier_semaphore()
    for device in peers:
        pl.semaphore_signal(barrier, inc=1, device_id=device, device_id_type=MESH)
    pl.semaphore_wait(barrier, len(peers))

    base_a, base_b = spans[3]
    first, second, third, fourth = [], [], [], []
    for q in range(4):
        pq, fq = part.at[q], proj.at[q]
        first.append((Reduce(links, rx, pq, 0, r1, x1.at[q]), Reduce(links, ry, pq, half, r1, y1.at[q])))
        second.append((Reduce(links, ry, pq, base_a, r2, y2.at[q]), Reduce(links, rx, pq, base_b, r2, x2.at[q])))
        third.append((Gather(links, ry, fq, base_a, r2), Gather(links, rx, fq, base_b, r2)))
        fourth.append((Gather(links, rx, fq, 0, r1), Gather(links, ry, fq, half, r1)))

    inv_cols = 1.0 / jnp.sqrt(jnp.float32(COLS))
    v_in.wait()
    vh[...], vl[...] = split(v_ref[...])
    for h in range(2):
        for j in range(4):
            if h == 0:
                for c in arrivals[j]:
                    c.wait()
                for at in spans[j]:
                    high, low = split(m_ref[pl.ds(at, r1), :] + g_ref[pl.ds(at, r1), :].astype(F32))
                    bh[pl.ds(at, r1), :] = high
                    bl[pl.ds(at, r1), :] = low
            highs = jnp.concatenate([bh[pl.ds(at, r1), :] for at in spans[j]])
            lows = jnp.concatenate([bl[pl.ds(at, r1), :] for at in spans[j]])
            col = slice(h * wide, (h + 1) * wide)
            value = dot3(highs, lows, vh[:, col], vl[:, col]) * inv_cols
            for i in range(2):
                q = 2 * h + i
                for l, at in enumerate(spans[j]):
                    part[q, pl.ds(at, r1), :] = value[l * r1:(l + 1) * r1, i * 128:(i + 1) * 128]
                if j < 3:
                    for one in first[q]:
                        one.send(j)

    for q in range(4):
        for one, two in zip(first[q], second[q]):
            one.chunk(one.g.me)[...] = one.finish()
            two.start()
    for q in range(4):
        for two, three in zip(second[q], third[q]):
            three.chunk(three.g.me)[...] = two.finish()
            three.start()
    for q in range(4):
        for three, four in zip(third[q], fourth[q]):
            three.finish()
            four.start()

    g0 = SumOver8(links, rz, core, partner, gram0, gpair0, gland0, gsum0)
    g1 = SumOver8(links, rz, core, partner, gram1, gpair1, gland1, gsum1)
    ws = [
        SumOver8(links, rz, core, partner, w.at[h], wpair.at[h], wland.at[h], wsum.at[h]) for h in range(2)
    ]

    def turned(h):
        step = 256
        for q in (2 * h, 2 * h + 1):
            for four in fourth[q]:
                four.finish()

            def body(i, c):
                at = pl.multiple_of(i * step, step)
                value = proj[q, pl.ds(at, step), :]
                col = slice(q * 128, (q + 1) * 128)
                ph[pl.ds(at, step), col], pl_[pl.ds(at, step), col] = split(value)
                pth[col, pl.ds(at, step)], ptl[col, pl.ds(at, step)] = split(value.T)
                return c

            lax.fori_loop(0, rows // step, body, 0)

    def products(h):
        col = slice(h * wide, (h + 1) * wide)
        w[h] = dot3(pth[col, :], ptl[col, :], bh[...], bl[...])

    turned(0)
    gram0[...] = dot3(pth[:wide, :], ptl[:wide, :], ph[:, :wide], pl_[:, :wide])
    g0.exchange()
    products(0)
    g0.begin()
    ws[0].exchange()
    turned(1)
    gram1[...] = dot3(pth[wide:, :], ptl[wide:, :], ph[...], pl_[...])
    g1.exchange()
    squares = jnp.zeros((8, 128), F32)
    for q in range(4):
        value = proj[q]
        squares = squares + jnp.sum((value * value).reshape(rows // 8, 8, 128), axis=0)
    tbuf[0] = squares
    tslots = [links.slot() for _ in range(4)]
    links.send(tslots[0], tbuf.at[0], tland.at[4], partner)
    g1.begin()
    links.landed(tslots[0], tland.at[4], partner)
    tland[z] = tbuf[0] + tland[4]
    for j in range(3):
        links.send(tslots[1 + j], tland.at[z], tland.at[z], rz.devices[j])
    g0.turn()
    products(1)
    ws[1].exchange()
    ws[0].begin()
    for j in range(3):
        links.landed(tslots[1 + j], tland.at[rz.sources[j]], rz.devices[j])
    shift = 0.0001 * jnp.sum(((tland[0] + tland[1]) + tland[2]) + tland[3]) / rank
    g0.forward()
    g0.end()

    rid = lax.broadcasted_iota(jnp.int32, (wide, wide), 0)
    cid = lax.broadcasted_iota(jnp.int32, (wide, wide), 1)
    diagonal = jnp.where(rid == cid, shift, 0.0)
    events = [None, g1.turn, ws[1].begin, None, ws[0].turn, g1.forward, g1.end, None,
              ws[1].turn, None, ws[0].forward, None, None, None, ws[1].forward, None]

    def event():
        e = events.pop(0)
        if e is not None:
            e()

    s0[...] = gsum0[...] + diagonal
    for k in range(wide // 128):
        factor_step(k, s0, a_ref, r_ref, t_ref, event)
    inv0 = jnp.where(cid <= rid, s0[...], 0.0)
    s0[...] = inv0
    low = full(gsum1[:, :wide], inv0, NT)
    s1[...] = gsum1[:, wide:] + diagonal - full(low, low, NT)
    s2[...] = full(low, inv0)
    for k in range(wide // 128):
        factor_step(k, s1, a_ref, r_ref, t_ref, event)
    inv1 = jnp.where(cid <= rid, s1[...], 0.0)
    x0h, x0l = split(s0[...])
    x1h, x1l = split(inv1)
    xch, xcl = split(-full(inv1, s2[...]))
    ws[0].end()
    ws[1].end()

    w0h, w0l = split(wsum[0])
    w1h, w1l = split(wsum[1])
    sums = []
    for h in range(2):
        col = slice(h * wide, (h + 1) * wide)
        if h == 0:
            back_t = dot3(x0h, x0l, w0h, w0l)
        else:
            back_t = dot3(xch, xcl, w0h, w0l) + dot3(x1h, x1l, w1h, w1l)
        bth_ref[col, :], btl_ref[col, :] = split(back_t)
        back = back_t.T
        basis_ref[:, col] = back
        sums.append(jnp.sum(back * back, axis=0, keepdims=True))
    total = jnp.concatenate(sums, axis=1)
    colsum[...] = jnp.broadcast_to(total, colsum.shape)
    cslots = [links.slot() for _ in plane]
    for o, device in enumerate(plane):
        links.send(cslots[o], colsum, cland.at[o], device)
    outs = [(bth_ref, bth_hbm), (btl_ref, btl_hbm), (basis_ref, basis_hbm)]
    copies = []

    def store(src, dst):
        copies.append(pltpu.make_async_copy(src, dst, out_sem.at[len(copies)]))
        copies[-1].start()

    for src, dst in outs:
        store(src, dst)
    oh_ref[:, :wide], ol_ref[:, :wide] = split(dot3(ph[:, :wide], pl_[:, :wide], x0h, x0l, NT))
    oh_ref[:, wide:], ol_ref[:, wide:] = split(
        dot3(ph[:, :wide], pl_[:, :wide], xch, xcl, NT) + dot3(ph[:, wide:], pl_[:, wide:], x1h, x1l, NT)
    )
    store(oh_ref, oh_hbm)
    store(ol_ref, ol_hbm)
    links.drain()
    for o, device in enumerate(plane):
        links.landed(cslots[o], cland.at[o], device)
        total = total + cland[o, 0:1, :]
    sc_ref[...] = jnp.broadcast_to(1.0 / jnp.sqrt(total / COLS + 1e-06), sc_ref.shape)
    store(sc_ref, sc_hbm)
    for c in copies:
        c.wait()


def kernel_outputs(m_ref, g_ref, oh_ref, ol_ref, bth_ref, btl_ref, b_ref, sc_ref, mo_ref, bo_ref, u_ref):
    buffer = m_ref[...] + g_ref[...].astype(F32)
    low = jnp.dot(oh_ref[...], bth_ref[...], preferred_element_type=F32)
    mo_ref[...] = buffer - 0.05 * low
    scale = sc_ref[0:1, :]
    ortho = oh_ref[...].astype(F32) + ol_ref[...].astype(F32)
    high, rest = split(ortho * (scale * jnp.sqrt(jnp.float32(ROWS) / RANK)))
    u_ref[...] = dot3(high, rest, bth_ref[...], btl_ref[...]).astype(BF16)
    bo_ref[...] = b_ref[...] * scale


def sums_call(momentum, gradient, basis):
    rows, cols = momentum.shape
    rank = basis.shape[1]
    r1, r2, wide = rows // 8, rows // 32, rank // 2

    def mem(shape, kind=F32):
        return pltpu.VMEM(shape, kind)

    def out(shape, kind=F32):
        return jax.ShapeDtypeStruct(shape, kind)

    outs = (
        ((rows, rank), BF16), ((rows, rank), BF16), ((rank, cols), BF16), ((rank, cols), BF16),
        ((cols, rank), F32), ((8, rank), F32),
    )
    n = wide // 8
    anywhere = pl.BlockSpec(memory_space=pl.ANY)
    return pl.pallas_call(
        kernel_sums,
        out_shape=tuple(out(*o) for o in outs),
        in_specs=[anywhere] * 3,
        out_specs=(anywhere,) * 6,
        scratch_shapes=[
            mem((rows, cols)), mem((rows, cols), BF16), mem((cols, rank)),
            *(mem(*o) for o in outs),
            mem((rows, cols), BF16), mem((rows, cols), BF16), mem((cols, rank), BF16), mem((cols, rank), BF16),
            mem((4, rows, 128)), mem((4, rows, 128)),
            mem((rows, rank), BF16), mem((rows, rank), BF16), mem((rank, rows), BF16), mem((rank, rows), BF16),
            mem((wide, wide)), mem((wide // 2, wide)), mem((3, n, wide)), mem((wide, wide)),
            mem((wide, rank)), mem((wide // 2, rank)), mem((3, n, rank)), mem((wide, rank)),
            mem((2, wide, cols)), mem((2, wide // 2, cols)), mem((2, 3, n, cols)), mem((2, wide, cols)),
            mem((wide, wide)), mem((wide, wide)), mem((wide, wide)),
            mem((136, 256)), mem((8, 256)), mem((136, 8)),
            mem((4, 3, r1, 128)), mem((4, 3, r1, 128)), mem((4, 3, r2, 128)), mem((4, 3, r2, 128)),
            mem((1, 8, 128)), mem((5, 8, 128)), mem((8, rank)), mem((15, 8, rank)),
            pltpu.SemaphoreType.DMA((17,)), pltpu.SemaphoreType.DMA((6,)),
            pltpu.SemaphoreType.DMA((160,)), pltpu.SemaphoreType.DMA((160,)),
        ],
        compiler_params=pltpu.CompilerParams(
            collective_id=0, has_side_effects=True, vmem_limit_bytes=62 * 2**20
        ),
        cost_estimate=pl.CostEstimate(flops=10 * 10**9, bytes_accessed=20 * 2**20, transcendentals=0),
    )(momentum, gradient, basis)


def shards(momentum, gradient, basis):
    rows, cols = momentum.shape
    rank = basis.shape[1]

    def out(shape, kind=F32):
        return jax.ShapeDtypeStruct(shape, kind)

    oh, ol, bth, btl, back, scale = sums_call(momentum, gradient, basis)
    tiles = 4
    tr, tc = rows // tiles, cols // tiles

    def rowed(width):
        return pl.BlockSpec((tr, width), lambda i: (i, 0))

    fixed = pl.BlockSpec((rank, cols), lambda i: (0, 0))
    cut_cols = pl.BlockSpec((tc, rank), lambda i: (i, 0))
    small = pl.BlockSpec((8, rank), lambda i: (0, 0))
    return pl.pallas_call(
        kernel_outputs,
        grid=(tiles,),
        out_shape=(out((rows, cols)), out((cols, rank)), out((rows, cols), BF16)),
        in_specs=[rowed(cols), rowed(cols), rowed(rank), rowed(rank), fixed, fixed, cut_cols, small],
        out_specs=(rowed(cols), cut_cols, rowed(cols)),
        compiler_params=pltpu.CompilerParams(vmem_limit_bytes=62 * 2**20),
        cost_estimate=pl.CostEstimate(flops=4 * 10**9, bytes_accessed=18 * 2**20, transcendentals=0),
    )(momentum, gradient, oh, ol, bth, btl, back, scale)


def solution(mesh):
    placed = (P("fsdp", "tp"), P("fsdp", "tp"), P("tp", None))
    return jax.shard_map(
        shards,
        mesh=mesh,
        in_specs=placed,
        out_specs=(P("fsdp", "tp"), P("tp", None), P("fsdp", "tp")),
        check_vma=False,
    )
```

```python
import functools

import jax
import jax.numpy as jnp
from jax import lax
from jax.experimental import pallas as pl
from jax.experimental.pallas import tpu as pltpu
from jax.sharding import PartitionSpec as P

ROWS = 8192
COLS = 14336
RANK = 512
HI = lax.Precision.HIGHEST
F32 = jnp.float32
BF16 = jnp.bfloat16
MESH = pl.DeviceIdType.MESH
NT = (((1,), (1,)), ((), ()))
TN = (((0,), (0,)), ((), ()))
NN = (((1,), (0,)), ((), ()))


def split(v):
    high = v.astype(BF16)
    return high, (v - high.astype(F32)).astype(BF16)


def dot3(ah, al, bh, bl, dims=NN):
    def one(a, b):
        return lax.dot_general(a, b, dims, preferred_element_type=F32)

    return one(ah, bl) + one(al, bh) + one(ah, bh)


class Links:
    def __init__(self, send_sem, recv_sem):
        self.send_sem, self.recv_sem, self.used, self.sent = send_sem, recv_sem, 0, []

    def slot(self):
        self.used += 1
        return self.used - 1

    def copy(self, slot, src, dst, device):
        return pltpu.make_async_remote_copy(
            src_ref=src,
            dst_ref=dst,
            send_sem=self.send_sem.at[slot],
            recv_sem=self.recv_sem.at[slot],
            device_id=device,
            device_id_type=MESH,
        )

    def send(self, slot, src, dst, device):
        c = self.copy(slot, src, dst, device)
        c.start()
        self.sent.append(c)

    def landed(self, slot, dst, device):
        self.copy(slot, dst, dst, device).wait_recv()

    def drain(self):
        for c in self.sent:
            c.wait_send()
        self.sent = []


class Ring:
    def __init__(self, me, at):
        self.me = me
        self.others = [lax.rem(me + o, 4) for o in (2, 1, 3)]
        self.devices = [at(i) for i in self.others]
        self.sources = [lax.rem(me + o, 4) for o in (2, 3, 1)]


def cut(ref, at, n):
    return ref.at[pl.ds(pl.multiple_of(at, n), n), :]


class Reduce:
    def __init__(self, links, ring, ref, base, rows, land):
        self.k, self.g, self.ref, self.base, self.rows, self.land = links, ring, ref, base, rows, land
        self.s = [links.slot() for _ in range(3)]

    def chunk(self, i):
        return cut(self.ref, self.base + i * self.rows, self.rows)

    def send(self, j):
        self.k.send(self.s[j], self.chunk(self.g.others[j]), self.land.at[j], self.g.devices[j])

    def start(self):
        for j in range(3):
            self.send(j)

    def finish(self):
        for j in range(3):
            self.k.landed(self.s[j], self.land.at[j], self.g.devices[j])
        return (self.chunk(self.g.me)[...] + self.land[0]) + (self.land[1] + self.land[2])


class Gather:
    def __init__(self, links, ring, ref, base, rows):
        self.k, self.g, self.ref, self.base, self.rows = links, ring, ref, base, rows
        self.s = [links.slot() for _ in range(3)]

    def chunk(self, i):
        return cut(self.ref, self.base + i * self.rows, self.rows)

    def start(self):
        own = self.chunk(self.g.me)
        for j in range(3):
            self.k.send(self.s[j], own, own, self.g.devices[j])

    def finish(self):
        for j in range(3):
            self.k.landed(self.s[j], self.chunk(self.g.sources[j]), self.g.devices[j])


class RelayReduce(Reduce):
    def __init__(self, links, ring, ref, base, rows, land):
        self.k, self.g, self.ref, self.base, self.rows, self.land = links, ring, ref, base, rows // 2, land
        self.s = [links.slot() for _ in range(6)]

    def half(self, i, h):
        return cut(self.ref, self.base + (2 * i + h) * self.rows, self.rows)

    def relay(self):
        for d in range(2):
            self.k.send(self.s[d], self.half(self.g.others[0], d), self.land.at[d], self.g.devices[1 + d])

    def direct(self):
        for d in range(2):
            part = self.half(self.g.others[1 + d], 1 - d)
            self.k.send(self.s[2 + d], part, self.land.at[2 + d], self.g.devices[1 + d])

    def start(self):
        self.relay()
        self.direct()

    def mid(self):
        for d in range(2):
            self.k.landed(self.s[d], self.land.at[d], self.g.devices[1 + d])
            part = self.half(self.g.others[1 + d], d)
            part[...] += self.land[d]
            self.k.send(self.s[4 + d], part, self.land.at[4 + d], self.g.devices[1 + d])

    def finish(self):
        for j in range(2, 6):
            self.k.landed(self.s[j], self.land.at[j], self.g.devices[1])
        own = [self.half(self.g.me, d)[...] + self.land[4 + d] + self.land[3 - d] for d in range(2)]
        return jnp.concatenate(own)

    def chunk(self, i):
        return cut(self.ref, self.base + i * 2 * self.rows, 2 * self.rows)


class RelayGather(Gather):
    def __init__(self, links, ring, ref, base, rows):
        super().__init__(links, ring, ref, base, rows)
        self.s.append(links.slot())

    def half(self, i, h):
        n = self.rows // 2
        return cut(self.ref, self.base + i * self.rows + h * n, n)

    def start(self):
        own = self.chunk(self.g.me)
        for d in range(2):
            self.k.send(self.s[d], own, own, self.g.devices[1 + d])

    def mid(self):
        for d in range(2):
            self.k.landed(self.s[d], self.chunk(self.g.sources[1 + d]), self.g.devices[1 + d])
            part = self.half(self.g.sources[1 + d], d)
            self.k.send(self.s[2 + d], part, part, self.g.devices[1 + d])

    def finish(self):
        for d in range(2):
            self.k.landed(self.s[2 + d], self.half(self.g.others[0], d), self.g.devices[1 + d])


class SumOver8:
    def __init__(self, links, ring, core, partner, ref, pair, land, total, relay=False):
        self.k, self.core, self.partner, self.ref, self.pair, self.total = links, core, partner, ref, pair, total
        self.ring = ring
        self.n = ref.shape[0] // 2
        self.rows = self.n // 4
        self.s = [links.slot() for _ in range(5)]
        self.base = core * self.n
        self.other = (1 - core) * self.n
        self.relay = relay
        self.reduce = (RelayReduce if relay else Reduce)(links, ring, ref, self.base, self.rows, land)
        self.gather = (RelayGather if relay else Gather)(links, ring, total, self.base, self.rows)

    def exchange(self):
        self.k.send(self.s[0], cut(self.ref, self.other, self.n), self.pair, self.partner)

    def begin(self):
        self.k.landed(self.s[0], self.pair, self.partner)
        own = cut(self.ref, self.base, self.n)
        own[...] += self.pair[...]
        self.reduce.start()

    def pass_on(self, j, chunk):
        part = self.gather.chunk(chunk)
        self.k.send(self.s[1 + j], part, part, self.partner)

    def turn(self):
        self.gather.chunk(self.ring.me)[...] = self.reduce.finish()
        self.gather.start()
        self.pass_on(0, self.ring.me)

    def mid(self):
        self.reduce.mid()

    def forward(self):
        if self.relay:
            self.gather.mid()
        else:
            self.last()
        for j in (1, 2):
            self.pass_on(1 + j, self.ring.sources[j])

    def last(self):
        self.gather.finish()
        self.pass_on(1, self.ring.sources[0])

    def end(self):
        for j, chunk in enumerate([self.ring.me] + self.ring.sources):
            self.k.landed(self.s[1 + j], cut(self.total, self.other + chunk * self.rows, self.rows), self.partner)


def lane(v, j):
    return jnp.take_along_axis(v, jnp.full(v.shape, j, jnp.int32), axis=1)


def row(v, j):
    return jnp.broadcast_to(v[j:j + 1, :], v.shape)


def tree(terms):
    while len(terms) > 1:
        terms = [terms[i] + terms[i + 1] for i in range(0, len(terms), 2)]
    return terms[0]


def eight(s, a_ref, r_ref, t_ref):
    sid = lax.broadcasted_iota(jnp.int32, (8, 128), 0)
    o = pl.multiple_of(8 * s, 8)
    on = pl.multiple_of(8 * s + 8, 8)
    p, q = a_ref[pl.ds(o, 8), 0:128], a_ref[pl.ds(o, 8), 128:256]
    n, nx = a_ref[pl.ds(on, 8), 0:128], a_ref[pl.ds(on, 8), 128:256]
    last = r_ref[...]
    t = t_ref[pl.ds(on, 8), :]
    terms, termsx = [], []
    for j in range(8):
        l = jnp.broadcast_to(t[:, j:j + 1], (8, 128))
        terms.append(l * row(last[:, 0:128], j))
        termsx.append(l * row(last[:, 128:256], j))
    n, nx = n - tree(terms), nx - tree(termsx)
    cb = [lane(p, 8 * s + j) for j in range(8)]
    cn = [lane(n, 8 * s + j) for j in range(8)]
    pivot = row(cb[0], 0)
    pivots = pivot
    for j in range(8):
        d = 1.0 / pivot
        cm = jnp.where(sid > j, cb[j], 0.0)
        if j < 7:
            e = row(cb[j], j + 1)
            pivot = row(cb[j + 1], j + 1) - (e * e) * d
            pivots = jnp.where(sid > j, pivot, pivots)
        for k in range(j + 1, 8):
            m = row(cb[k], j)
            cb[k] = cb[k] - (cm * m) * d
            cn[k] = cn[k] - cn[j] * (m * d)
        u, ux = row(p, j) * d, row(q, j) * d
        p, q = p - cm * u, q - cm * ux
        n, nx = n - cn[j] * u, nx - cn[j] * ux
    scale = lax.rsqrt(pivots)
    p, q = p * scale, q * scale
    rest = jnp.dot(t_ref[0:128, :], last, precision=HI, preferred_element_type=F32)
    rid = lax.broadcasted_iota(jnp.int32, (128, 256), 0)
    a_ref[0:128, :] -= jnp.where(rid >= 8 * s + 16, rest, 0.0)
    a_ref[pl.ds(o, 8), 128:256] = q
    a_ref[pl.ds(on, 8), 0:128] = n
    a_ref[pl.ds(on, 8), 128:256] = nx
    r_ref[:, 0:128] = p
    r_ref[:, 128:256] = q
    t_ref[0:128, :] = p.T


def factor_step(k, s_ref, a_ref, r_ref, t_ref, event):
    n = s_ref.shape[0]
    o = 128 * k
    i128 = lax.broadcasted_iota(jnp.int32, (128, 128), 0)
    j128 = lax.broadcasted_iota(jnp.int32, (128, 128), 1)
    unit = jnp.where(i128 == j128, 1.0, 0.0).astype(F32)
    a_ref[0:128, 0:128] = s_ref[o:o + 128, o:o + 128]
    a_ref[0:128, 128:256] = unit
    a_ref[128:136, :] = jnp.zeros((8, 256), F32)
    r_ref[...] = jnp.zeros(r_ref.shape, F32)
    t_ref[...] = jnp.zeros(t_ref.shape, F32)

    def body(s, c):
        eight(s, a_ref, r_ref, t_ref)
        return c

    for quarter in range(4):
        lax.fori_loop(4 * quarter, 4 * quarter + 4, body, 0)
        event()
    s_ref[o:o + 128, o:o + 128] = unit
    block = jnp.dot(a_ref[0:128, 128:256], s_ref[o:o + 128, :], precision=HI, preferred_element_type=F32)
    s_ref[o:o + 128, :] = block
    if o + 128 < n:
        s_ref[o + 128:, o:o + 128] = jnp.zeros((n - o - 128, 128), F32)
        s_ref[o + 128:, :] -= lax.dot_general(
            block[:, o + 128:], block, TN, precision=HI, preferred_element_type=F32
        )


def full(a, b, dims=NN):
    return lax.dot_general(a, b, dims, precision=HI, preferred_element_type=F32)


def kernel_sums(
    m_hbm, g_hbm, v_hbm,
    oh_hbm, ol_hbm, bth_hbm, btl_hbm, basis_hbm, sc_hbm, mo_hbm,
    m_ref, g_ref, v_ref, oh_ref, ol_ref, bth_ref, btl_ref, basis_ref, sc_ref,
    bh, bl, vh, vl, part, proj, ph, pl_, pth, ptl,
    gram0, gpair0, gland0, gsum0, gram1, gpair1, gland1, gsum1, w, wpair, wland, wsum,
    s0, s1, s2, a_ref, r_ref, t_ref, x1, y1, y2, x2, tbuf, tland, colsum, cland,
    in_sem, out_sem, send_sem, recv_sem,
):
    f, t = lax.axis_index("fsdp"), lax.axis_index("tp")
    z, core = lax.div(f, 2), lax.rem(f, 2)
    x, y = lax.div(t, 4), lax.rem(t, 4)
    rows = m_ref.shape[0]
    rank = v_ref.shape[1]
    half, r1, r2 = rows // 2, rows // 8, rows // 32
    wide = rank // 2

    rx = Ring(x, lambda i: (f, i * 4 + y))
    ry = Ring(y, lambda i: (f, x * 4 + i))
    rz = Ring(z, lambda i: (i * 2 + core, t))
    partner = (f + 1 - 2 * core, t)
    plane = [(f, lax.rem(t + o, 16)) for o in range(1, 16)]
    links = Links(send_sem, recv_sem)
    peers = plane + rz.devices + [partner]
    barrier = pltpu.get_barrier_semaphore()
    for device in peers:
        pl.semaphore_signal(barrier, inc=1, device_id=device, device_id_type=MESH)

    v_in = pltpu.make_async_copy(v_hbm, v_ref, in_sem.at[0])
    v_in.start()
    spans, arrivals = [], []
    for j, d in enumerate((2, 1, 3, 0)):
        pair = (
            pl.multiple_of(lax.rem(x + d, 4) * r1, r1),
            pl.multiple_of(half + lax.rem(y + d, 4) * r1, r1),
        )
        spans.append(pair)
        arrivals.append([])
        for i, at in enumerate(pair):
            for l, (src, dst) in enumerate(((m_hbm, m_ref), (g_hbm, g_ref))):
                c = pltpu.make_async_copy(
                    src.at[pl.ds(at, r1), :], dst.at[pl.ds(at, r1), :], in_sem.at[1 + 4 * j + 2 * i + l]
                )
                c.start()
                arrivals[-1].append(c)

    base_a, base_b = spans[3]
    first, second, third, fourth = [], [], [], []
    for q in range(4):
        pq, fq = part.at[q], proj.at[q]
        first.append((RelayReduce(links, rx, pq, 0, r1, x1.at[q]), RelayReduce(links, ry, pq, half, r1, y1.at[q])))
        second.append((Reduce(links, ry, pq, base_a, r2, y2.at[q]), Reduce(links, rx, pq, base_b, r2, x2.at[q])))
        third.append((Gather(links, ry, fq, base_a, r2), Gather(links, rx, fq, base_b, r2)))
        fourth.append((RelayGather(links, rx, fq, 0, r1), RelayGather(links, ry, fq, half, r1)))

    def add(q):
        for one in first[q]:
            one.mid()

    inv_cols = 1.0 / jnp.sqrt(jnp.float32(COLS))
    v_in.wait()
    vh[...], vl[...] = split(v_ref[...])
    for h in range(2):
        for j in range(4):
            if h == 0:
                for c in arrivals[j]:
                    c.wait()
                for at in spans[j]:
                    high, low = split(m_ref[pl.ds(at, r1), :] + g_ref[pl.ds(at, r1), :].astype(F32))
                    bh[pl.ds(at, r1), :] = high
                    bl[pl.ds(at, r1), :] = low
            highs = jnp.concatenate([bh[pl.ds(at, r1), :] for at in spans[j]])
            lows = jnp.concatenate([bl[pl.ds(at, r1), :] for at in spans[j]])
            col = slice(h * wide, (h + 1) * wide)
            value = dot3(highs, lows, vh[:, col], vl[:, col]) * inv_cols
            for i in range(2):
                q = 2 * h + i
                for l, at in enumerate(spans[j]):
                    part[q, pl.ds(at, r1), :] = value[l * r1:(l + 1) * r1, i * 128:(i + 1) * 128]
                if h == 0 and j == 0 and i == 0:
                    pl.semaphore_wait(barrier, len(peers))
                for one in first[q]:
                    if j == 0:
                        one.relay()
                    if j == 2:
                        one.direct()
            if h == 1 and j == 2:
                add(0)
                add(1)

    def step1(q):
        for one, two in zip(first[q], second[q]):
            one.chunk(one.g.me)[...] = one.finish()
            two.start()

    def step2(q):
        for two, three in zip(second[q], third[q]):
            three.chunk(three.g.me)[...] = two.finish()
            three.start()

    def step3(q):
        for three, four in zip(third[q], fourth[q]):
            three.finish()
            four.start()

    def step4(q):
        for four in fourth[q]:
            four.mid()

    add(2)
    add(3)
    for stage in (step1, step2, step3, step4):
        for q in range(4):
            stage(q)

    g0 = SumOver8(links, rz, core, partner, gram0, gpair0, gland0, gsum0)
    g1 = SumOver8(links, rz, core, partner, gram1, gpair1, gland1, gsum1)
    ws = [
        SumOver8(links, rz, core, partner, w.at[h], wpair.at[h], wland.at[h], wsum.at[h], True) for h in range(2)
    ]

    def turned(q):
        step = 256
        for four in fourth[q]:
            four.finish()
        col = slice(q * 128, (q + 1) * 128)

        def body(i, c):
            at = pl.multiple_of(i * step, step)
            value = proj[q, pl.ds(at, step), :]
            ph[pl.ds(at, step), col], pl_[pl.ds(at, step), col] = split(value)
            pth[col, pl.ds(at, step)], ptl[col, pl.ds(at, step)] = split(value.T)
            return c + jnp.sum((value * value).reshape(step // 8, 8, 128), axis=0)

        return lax.fori_loop(0, rows // step, body, jnp.zeros((8, 128), F32))

    def products(h, i):
        at = h * wide + i * 128
        col = slice(at, at + 128)
        w[h, i * 128:(i + 1) * 128, :] = dot3(pth[col, :], ptl[col, :], bh[...], bl[...])

    squares = turned(0)
    squares = squares + turned(1)
    gram0[...] = dot3(pth[:wide, :], ptl[:wide, :], ph[:, :wide], pl_[:, :wide])
    g0.exchange()
    squares = squares + turned(2)
    g0.begin()
    squares = squares + turned(3)
    tbuf[0] = squares
    tslots = [links.slot() for _ in range(4)]
    links.send(tslots[0], tbuf.at[0], tland.at[4], partner)
    gram1[...] = dot3(pth[wide:, :], ptl[wide:, :], ph[...], pl_[...])
    g1.exchange()
    links.landed(tslots[0], tland.at[4], partner)
    tland[z] = tbuf[0] + tland[4]
    for j in range(3):
        links.send(tslots[1 + j], tland.at[z], tland.at[z], rz.devices[j])
    g0.turn()
    products(0, 0)
    g1.begin()
    products(0, 1)
    ws[0].exchange()
    products(1, 0)
    ws[0].begin()
    products(1, 1)
    ws[1].exchange()
    g0.forward()
    for j in range(3):
        links.landed(tslots[1 + j], tland.at[rz.sources[j]], rz.devices[j])
    shift = 0.0001 * jnp.sum(((tland[0] + tland[1]) + tland[2]) + tland[3]) / rank
    g0.end()

    rid = lax.broadcasted_iota(jnp.int32, (wide, wide), 0)
    cid = lax.broadcasted_iota(jnp.int32, (wide, wide), 1)
    diagonal = jnp.where(rid == cid, shift, 0.0)
    events = [g1.turn, ws[0].mid, ws[1].begin, None, g1.forward, ws[0].turn, g1.end, ws[1].mid,
              ws[0].forward, ws[1].turn, None, ws[0].last, None, ws[1].forward, None, None]

    def event():
        e = events.pop(0)
        if e is not None:
            e()

    s0[...] = gsum0[...] + diagonal
    for k in range(wide // 128):
        factor_step(k, s0, a_ref, r_ref, t_ref, event)
    inv0 = jnp.where(cid <= rid, s0[...], 0.0)
    s0[...] = inv0
    low = full(gsum1[:, :wide], inv0, NT)
    s1[...] = gsum1[:, wide:] + diagonal - full(low, low, NT)
    s2[...] = full(low, inv0)
    for k in range(wide // 128):
        factor_step(k, s1, a_ref, r_ref, t_ref, event)
    inv1 = jnp.where(cid <= rid, s1[...], 0.0)
    x0h, x0l = split(s0[...])
    x1h, x1l = split(inv1)
    xch, xcl = split(-full(inv1, s2[...]))
    ws[1].last()
    ws[0].end()
    ws[1].end()

    w0h, w0l = split(wsum[0])
    w1h, w1l = split(wsum[1])
    sums = []
    for h in range(2):
        col = slice(h * wide, (h + 1) * wide)
        if h == 0:
            back_t = dot3(x0h, x0l, w0h, w0l)
        else:
            back_t = dot3(xch, xcl, w0h, w0l) + dot3(x1h, x1l, w1h, w1l)
        bth_ref[col, :], btl_ref[col, :] = split(back_t)
        back = back_t.T
        basis_ref[:, col] = back
        sums.append(jnp.sum(back * back, axis=0, keepdims=True))
    total = jnp.concatenate(sums, axis=1)
    colsum[...] = jnp.broadcast_to(total, colsum.shape)
    cslots = [links.slot() for _ in plane]
    for o, device in enumerate(plane):
        links.send(cslots[o], colsum, cland.at[o], device)
    outs = [(bth_ref, bth_hbm), (btl_ref, btl_hbm), (basis_ref, basis_hbm)]
    copies = []

    def store(src, dst):
        copies.append(pltpu.make_async_copy(src, dst, out_sem.at[len(copies)]))
        copies[-1].start()

    for src, dst in outs:
        store(src, dst)
    oh_ref[:, :wide], ol_ref[:, :wide] = split(dot3(ph[:, :wide], pl_[:, :wide], x0h, x0l, NT))
    oh_ref[:, wide:], ol_ref[:, wide:] = split(
        dot3(ph[:, :wide], pl_[:, :wide], xch, xcl, NT) + dot3(ph[:, wide:], pl_[:, wide:], x1h, x1l, NT)
    )
    store(oh_ref, oh_hbm)
    store(ol_ref, ol_hbm)
    for i in range(4):
        at = slice(i * rows // 4, (i + 1) * rows // 4)
        low = jnp.dot(oh_ref[at, :], bth_ref[...], preferred_element_type=F32)
        m_ref[at, :] = m_ref[at, :] + g_ref[at, :].astype(F32) - 0.05 * low
        store(m_ref.at[at, :], mo_hbm.at[at, :])
    links.drain()
    for o, device in enumerate(plane):
        links.landed(cslots[o], cland.at[o], device)
        total = total + cland[o, 0:1, :]
    sc_ref[...] = jnp.broadcast_to(1.0 / jnp.sqrt(total / COLS + 1e-06), sc_ref.shape)
    store(sc_ref, sc_hbm)
    for c in copies:
        c.wait()


def kernel_outputs(mi_ref, oh_ref, ol_ref, bth_ref, btl_ref, b_ref, sc_ref, mo_ref, bo_ref, u_ref):
    scale = sc_ref[0:1, :]
    ortho = oh_ref[...].astype(F32) + ol_ref[...].astype(F32)
    high, rest = split(ortho * (scale * jnp.sqrt(jnp.float32(ROWS) / RANK)))
    mo_ref[...] = mi_ref[...]
    u_ref[...] = dot3(high, rest, bth_ref[...], btl_ref[...]).astype(BF16)
    bo_ref[...] = b_ref[...] * scale


def sums_call(momentum, gradient, basis):
    rows, cols = momentum.shape
    rank = basis.shape[1]
    r1, r2, wide = rows // 8, rows // 32, rank // 2

    def mem(shape, kind=F32):
        return pltpu.VMEM(shape, kind)

    def out(shape, kind=F32):
        return jax.ShapeDtypeStruct(shape, kind)

    outs = (
        ((rows, rank), BF16), ((rows, rank), BF16), ((rank, cols), BF16), ((rank, cols), BF16),
        ((cols, rank), F32), ((8, rank), F32),
    )
    result = out((rows, cols))
    n = wide // 8
    anywhere = pl.BlockSpec(memory_space=pl.ANY)
    return pl.pallas_call(
        kernel_sums,
        out_shape=tuple(out(*o) for o in outs) + (result,),
        in_specs=[anywhere] * 3,
        out_specs=(anywhere,) * 7,
        scratch_shapes=[
            mem((rows, cols)), mem((rows, cols), BF16), mem((cols, rank)),
            *(mem(*o) for o in outs),
            mem((rows, cols), BF16), mem((rows, cols), BF16), mem((cols, rank), BF16), mem((cols, rank), BF16),
            mem((4, rows, 128)), mem((4, rows, 128)),
            mem((rows, rank), BF16), mem((rows, rank), BF16), mem((rank, rows), BF16), mem((rank, rows), BF16),
            mem((wide, wide)), mem((wide // 2, wide)), mem((3, n, wide)), mem((wide, wide)),
            mem((wide, rank)), mem((wide // 2, rank)), mem((3, n, rank)), mem((wide, rank)),
            mem((2, wide, cols)), mem((2, wide // 2, cols)), mem((2, 6, n // 2, cols)), mem((2, wide, cols)),
            mem((wide, wide)), mem((wide, wide)), mem((wide, wide)),
            mem((136, 256)), mem((8, 256)), mem((136, 8)),
            mem((4, 6, r1 // 2, 128)), mem((4, 6, r1 // 2, 128)), mem((4, 3, r2, 128)), mem((4, 3, r2, 128)),
            mem((1, 8, 128)), mem((5, 8, 128)), mem((8, rank)), mem((15, 8, rank)),
            pltpu.SemaphoreType.DMA((17,)), pltpu.SemaphoreType.DMA((10,)),
            pltpu.SemaphoreType.DMA((208,)), pltpu.SemaphoreType.DMA((208,)),
        ],
        compiler_params=pltpu.CompilerParams(
            collective_id=0, has_side_effects=True, vmem_limit_bytes=62 * 2**20
        ),
        cost_estimate=pl.CostEstimate(flops=10 * 10**9, bytes_accessed=20 * 2**20, transcendentals=0),
    )(momentum, gradient, basis)


def shards(momentum, gradient, basis):
    rows, cols = momentum.shape
    rank = basis.shape[1]

    def out(shape, kind=F32):
        return jax.ShapeDtypeStruct(shape, kind)

    oh, ol, bth, btl, back, scale, corrected = sums_call(momentum, gradient, basis)
    tiles = 4
    tr, tc = rows // tiles, cols // tiles

    def rowed(width):
        return pl.BlockSpec((tr, width), lambda i: (i, 0))

    fixed = pl.BlockSpec((rank, cols), lambda i: (0, 0))
    cut_cols = pl.BlockSpec((tc, rank), lambda i: (i, 0))
    small = pl.BlockSpec((8, rank), lambda i: (0, 0))
    return pl.pallas_call(
        kernel_outputs,
        grid=(tiles,),
        out_shape=(out((rows, cols)), out((cols, rank)), out((rows, cols), BF16)),
        in_specs=[rowed(cols), rowed(rank), rowed(rank), fixed, fixed, cut_cols, small],
        out_specs=(rowed(cols), cut_cols, rowed(cols)),
        compiler_params=pltpu.CompilerParams(vmem_limit_bytes=62 * 2**20),
        cost_estimate=pl.CostEstimate(flops=4 * 10**9, bytes_accessed=18 * 2**20, transcendentals=0),
    )(corrected, oh, ol, bth, btl, back, scale)


def solution(mesh):
    placed = (P("fsdp", "tp"), P("fsdp", "tp"), P("tp", None))
    return jax.shard_map(
        shards,
        mesh=mesh,
        in_specs=placed,
        out_specs=(P("fsdp", "tp"), P("tp", None), P("fsdp", "tp")),
        check_vma=False,
    )
```

```python
import functools

import jax
import jax.numpy as jnp
from jax import lax
from jax.experimental import pallas as pl
from jax.experimental.pallas import tpu as pltpu
from jax.sharding import PartitionSpec as P

ROWS = 8192
COLS = 14336
RANK = 512
HI = lax.Precision.HIGHEST
F32 = jnp.float32
BF16 = jnp.bfloat16
MESH = pl.DeviceIdType.MESH
NT = (((1,), (1,)), ((), ()))
TN = (((0,), (0,)), ((), ()))
NN = (((1,), (0,)), ((), ()))


def split(v):
    high = v.astype(BF16)
    return high, (v - high.astype(F32)).astype(BF16)


def dot3(ah, al, bh, bl, dims=NN):
    def one(a, b):
        return lax.dot_general(a, b, dims, preferred_element_type=F32)

    return one(ah, bl) + one(al, bh) + one(ah, bh)


class Links:
    def __init__(self, send_sem, recv_sem):
        self.send_sem, self.recv_sem, self.used, self.sent = send_sem, recv_sem, 0, []

    def slot(self):
        self.used += 1
        return self.used - 1

    def copy(self, slot, src, dst, device):
        return pltpu.make_async_remote_copy(
            src_ref=src,
            dst_ref=dst,
            send_sem=self.send_sem.at[slot],
            recv_sem=self.recv_sem.at[slot],
            device_id=device,
            device_id_type=MESH,
        )

    def send(self, slot, src, dst, device):
        c = self.copy(slot, src, dst, device)
        c.start()
        self.sent.append(c)

    def landed(self, slot, dst, device):
        self.copy(slot, dst, dst, device).wait_recv()

    def drain(self):
        for c in self.sent:
            c.wait_send()
        self.sent = []


class Ring:
    def __init__(self, me, at):
        self.me = me
        self.others = [lax.rem(me + o, 4) for o in (2, 1, 3)]
        self.devices = [at(i) for i in self.others]
        self.sources = [lax.rem(me + o, 4) for o in (2, 3, 1)]


def cut(ref, at, n):
    return ref.at[pl.ds(pl.multiple_of(at, n), n), :]


class Reduce:
    def __init__(self, links, ring, ref, base, rows, land):
        self.k, self.g, self.ref, self.base, self.rows, self.land = links, ring, ref, base, rows, land
        self.s = [links.slot() for _ in range(3)]

    def chunk(self, i):
        return cut(self.ref, self.base + i * self.rows, self.rows)

    def send(self, j):
        self.k.send(self.s[j], self.chunk(self.g.others[j]), self.land.at[j], self.g.devices[j])

    def start(self):
        for j in range(3):
            self.send(j)

    def finish(self):
        for j in range(3):
            self.k.landed(self.s[j], self.land.at[j], self.g.devices[j])
        return (self.chunk(self.g.me)[...] + self.land[0]) + (self.land[1] + self.land[2])


class Gather:
    def __init__(self, links, ring, ref, base, rows):
        self.k, self.g, self.ref, self.base, self.rows = links, ring, ref, base, rows
        self.s = [links.slot() for _ in range(3)]

    def chunk(self, i):
        return cut(self.ref, self.base + i * self.rows, self.rows)

    def start(self):
        own = self.chunk(self.g.me)
        for j in range(3):
            self.k.send(self.s[j], own, own, self.g.devices[j])

    def finish(self):
        for j in range(3):
            self.k.landed(self.s[j], self.chunk(self.g.sources[j]), self.g.devices[j])


class RelayReduce(Reduce):
    def __init__(self, links, ring, ref, base, rows, land):
        self.k, self.g, self.ref, self.base, self.rows, self.land = links, ring, ref, base, rows // 2, land
        self.s = [links.slot() for _ in range(6)]

    def half(self, i, h):
        return cut(self.ref, self.base + (2 * i + h) * self.rows, self.rows)

    def relay(self):
        for d in range(2):
            self.k.send(self.s[d], self.half(self.g.others[0], d), self.land.at[d], self.g.devices[1 + d])

    def direct(self):
        for d in range(2):
            part = self.half(self.g.others[1 + d], 1 - d)
            self.k.send(self.s[2 + d], part, self.land.at[2 + d], self.g.devices[1 + d])

    def start(self):
        self.relay()
        self.direct()

    def mid(self):
        for d in range(2):
            self.k.landed(self.s[d], self.land.at[d], self.g.devices[1 + d])
            part = self.half(self.g.others[1 + d], d)
            part[...] += self.land[d]
            self.k.send(self.s[4 + d], part, self.land.at[4 + d], self.g.devices[1 + d])

    def finish(self):
        for j in range(2, 6):
            self.k.landed(self.s[j], self.land.at[j], self.g.devices[1])
        own = [self.half(self.g.me, d)[...] + self.land[4 + d] + self.land[3 - d] for d in range(2)]
        return jnp.concatenate(own)

    def chunk(self, i):
        return cut(self.ref, self.base + i * 2 * self.rows, 2 * self.rows)


class RelayGather(Gather):
    def __init__(self, links, ring, ref, base, rows):
        super().__init__(links, ring, ref, base, rows)
        self.s.append(links.slot())

    def half(self, i, h):
        n = self.rows // 2
        return cut(self.ref, self.base + i * self.rows + h * n, n)

    def start(self):
        own = self.chunk(self.g.me)
        for d in range(2):
            self.k.send(self.s[d], own, own, self.g.devices[1 + d])

    def mid(self):
        for d in range(2):
            self.k.landed(self.s[d], self.chunk(self.g.sources[1 + d]), self.g.devices[1 + d])
            part = self.half(self.g.sources[1 + d], d)
            self.k.send(self.s[2 + d], part, part, self.g.devices[1 + d])

    def finish(self):
        for d in range(2):
            self.k.landed(self.s[2 + d], self.half(self.g.others[0], d), self.g.devices[1 + d])


class SumOver8:
    def __init__(self, links, ring, core, partner, ref, pair, land, total, relay=False, relay_back=False):
        self.k, self.core, self.partner, self.ref, self.pair, self.total = links, core, partner, ref, pair, total
        self.ring = ring
        self.n = ref.shape[0] // 2
        self.rows = self.n // 4
        self.s = [links.slot() for _ in range(5)]
        self.base = core * self.n
        self.other = (1 - core) * self.n
        self.relay_back = relay_back
        self.reduce = (RelayReduce if relay else Reduce)(links, ring, ref, self.base, self.rows, land)
        self.gather = (RelayGather if relay_back else Gather)(links, ring, total, self.base, self.rows)

    def exchange(self):
        self.k.send(self.s[0], cut(self.ref, self.other, self.n), self.pair, self.partner)

    def begin(self):
        self.k.landed(self.s[0], self.pair, self.partner)
        own = cut(self.ref, self.base, self.n)
        own[...] += self.pair[...]
        self.reduce.start()

    def pass_on(self, j, chunk):
        part = self.gather.chunk(chunk)
        self.k.send(self.s[1 + j], part, part, self.partner)

    def turn(self):
        self.gather.chunk(self.ring.me)[...] = self.reduce.finish()
        self.gather.start()
        self.pass_on(0, self.ring.me)

    def mid(self):
        self.reduce.mid()

    def forward(self):
        if self.relay_back:
            self.gather.mid()
        else:
            self.last()
        for j in (1, 2):
            self.pass_on(1 + j, self.ring.sources[j])

    def last(self):
        self.gather.finish()
        self.pass_on(1, self.ring.sources[0])

    def end(self):
        for j, chunk in enumerate([self.ring.me] + self.ring.sources):
            self.k.landed(self.s[1 + j], cut(self.total, self.other + chunk * self.rows, self.rows), self.partner)


def lane(v, j):
    return jnp.take_along_axis(v, jnp.full(v.shape, j, jnp.int32), axis=1)


def row(v, j):
    return jnp.broadcast_to(v[j:j + 1, :], v.shape)


def tree(terms):
    while len(terms) > 1:
        terms = [terms[i] + terms[i + 1] for i in range(0, len(terms), 2)]
    return terms[0]


def eight(s, a_ref, d_ref, r_ref, t_ref):
    sid = lax.broadcasted_iota(jnp.int32, (8, 128), 0)
    lid = lax.broadcasted_iota(jnp.int32, (8, 128), 1) - 8 * s
    o = pl.multiple_of(8 * s, 8)
    on = pl.multiple_of(8 * s + 8, 8)
    p, n = a_ref[pl.ds(o, 8), :], a_ref[pl.ds(on, 8), :]
    last = r_ref[...]
    t = t_ref[pl.ds(on, 8), :]
    before = (lid >= -8) & (lid < 0)
    now = (lid >= 0) & (lid < 8)
    terms = [jnp.broadcast_to(t[:, j:j + 1], (8, 128)) * row(last, j) for j in range(8)]
    n = jnp.where(before, 0.0, n) - tree(terms)
    cb = [lane(p, 8 * s + j) for j in range(8)]
    cn = [lane(n, 8 * s + j) for j in range(8)]
    p = jnp.where(now, jnp.where(lid == sid, 1.0, 0.0), p)
    n = jnp.where(now, 0.0, n)
    pivot = row(cb[0], 0)
    pivots = pivot
    for j in range(8):
        d = 1.0 / pivot
        cm = jnp.where(sid > j, cb[j], 0.0)
        if j < 7:
            e = row(cb[j], j + 1)
            pivot = row(cb[j + 1], j + 1) - (e * e) * d
            pivots = jnp.where(sid > j, pivot, pivots)
        for k in range(j + 1, 8):
            m = row(cb[k], j)
            cb[k] = cb[k] - (cm * m) * d
            cn[k] = cn[k] - cn[j] * (m * d)
        u = row(p, j) * d
        p, n = p - cm * u, n - cn[j] * u
    p = p * lax.rsqrt(pivots)
    rest = jnp.dot(t_ref[0:128, :], last, precision=HI, preferred_element_type=F32)
    lids = lax.broadcasted_iota(jnp.int32, (128, 128), 1) - 8 * s
    a_ref[0:128, :] = jnp.where((lids >= -8) & (lids < 0), 0.0, a_ref[0:128, :]) - rest
    a_ref[pl.ds(on, 8), :] = n
    d_ref[pl.ds(o, 8), :] = p
    r_ref[...] = p
    t_ref[0:128, :] = p.T


def factor_step(k, s_ref, a_ref, d_ref, r_ref, t_ref, event):
    n = s_ref.shape[0]
    o = 128 * k
    i128 = lax.broadcasted_iota(jnp.int32, (128, 128), 0)
    j128 = lax.broadcasted_iota(jnp.int32, (128, 128), 1)
    unit = jnp.where(i128 == j128, 1.0, 0.0).astype(F32)
    a_ref[0:128, :] = s_ref[o:o + 128, o:o + 128]
    a_ref[128:136, :] = jnp.zeros((8, 128), F32)
    r_ref[...] = jnp.zeros(r_ref.shape, F32)
    t_ref[...] = jnp.zeros(t_ref.shape, F32)

    def body(s, c):
        eight(s, a_ref, d_ref, r_ref, t_ref)
        return c

    for quarter in range(4):
        lax.fori_loop(4 * quarter, 4 * quarter + 4, body, 0)
        event()
    s_ref[o:o + 128, o:o + 128] = unit
    block = jnp.dot(jnp.where(j128 <= i128, d_ref[...], 0.0), s_ref[o:o + 128, :], precision=HI, preferred_element_type=F32)
    s_ref[o:o + 128, :] = block
    if o + 128 < n:
        s_ref[o + 128:, o:o + 128] = jnp.zeros((n - o - 128, 128), F32)
        s_ref[o + 128:, :] -= lax.dot_general(
            block[:, o + 128:], block, TN, precision=HI, preferred_element_type=F32
        )


def full(a, b, dims=NN):
    return lax.dot_general(a, b, dims, precision=HI, preferred_element_type=F32)


def kernel_sums(
    m_hbm, g_hbm, v_hbm,
    oh_hbm, ol_hbm, bth_hbm, btl_hbm, basis_hbm, sc_hbm, mo_hbm,
    m_ref, g_ref, v_ref, oh_ref, ol_ref, bth_ref, btl_ref, basis_ref, sc_ref,
    bh, bl, vh, vl, part, proj, ph, pl_, pth, ptl,
    gram0, gpair0, gland0, gsum0, gram1, gpair1, gland1, gsum1, w, wpair, wland, wsum,
    s0, s1, s2, a_ref, d_ref, r_ref, t_ref, x1, y1, y2, x2, tbuf, tland, colsum, cland,
    in_sem, out_sem, send_sem, recv_sem,
):
    f, t = lax.axis_index("fsdp"), lax.axis_index("tp")
    z, core = lax.div(f, 2), lax.rem(f, 2)
    x, y = lax.div(t, 4), lax.rem(t, 4)
    rows = m_ref.shape[0]
    rank = v_ref.shape[1]
    half, r1, r2 = rows // 2, rows // 8, rows // 32
    wide = rank // 2

    rx = Ring(x, lambda i: (f, i * 4 + y))
    ry = Ring(y, lambda i: (f, x * 4 + i))
    rz = Ring(z, lambda i: (i * 2 + core, t))
    partner = (f + 1 - 2 * core, t)
    plane = [(f, lax.rem(t + o, 16)) for o in range(1, 16)]
    links = Links(send_sem, recv_sem)
    peers = plane + rz.devices + [partner]
    barrier = pltpu.get_barrier_semaphore()
    for device in peers:
        pl.semaphore_signal(barrier, inc=1, device_id=device, device_id_type=MESH)

    v_in = pltpu.make_async_copy(v_hbm, v_ref, in_sem.at[0])
    v_in.start()
    spans, arrivals = [], []
    for j, d in enumerate((2, 1, 3, 0)):
        pair = (
            pl.multiple_of(lax.rem(x + d, 4) * r1, r1),
            pl.multiple_of(half + lax.rem(y + d, 4) * r1, r1),
        )
        spans.append(pair)
        arrivals.append([])
        for i, at in enumerate(pair):
            for l, (src, dst) in enumerate(((m_hbm, m_ref), (g_hbm, g_ref))):
                c = pltpu.make_async_copy(
                    src.at[pl.ds(at, r1), :], dst.at[pl.ds(at, r1), :], in_sem.at[1 + 4 * j + 2 * i + l]
                )
                c.start()
                arrivals[-1].append(c)

    base_a, base_b = spans[3]
    first, second, third, fourth = [], [], [], []
    for q in range(4):
        pq, fq = part.at[q], proj.at[q]
        first.append((RelayReduce(links, rx, pq, 0, r1, x1.at[q]), RelayReduce(links, ry, pq, half, r1, y1.at[q])))
        second.append((Reduce(links, ry, pq, base_a, r2, y2.at[q]), Reduce(links, rx, pq, base_b, r2, x2.at[q])))
        third.append((Gather(links, ry, fq, base_a, r2), Gather(links, rx, fq, base_b, r2)))
        fourth.append((Gather(links, rx, fq, 0, r1), Gather(links, ry, fq, half, r1)))

    def add(q):
        for one in first[q]:
            one.mid()

    inv_cols = 1.0 / jnp.sqrt(jnp.float32(COLS))
    v_in.wait()
    vh[...], vl[...] = split(v_ref[...])
    for h in range(2):
        for j in range(4):
            if h == 0:
                for c in arrivals[j]:
                    c.wait()
                for at in spans[j]:
                    high, low = split(m_ref[pl.ds(at, r1), :] + g_ref[pl.ds(at, r1), :].astype(F32))
                    bh[pl.ds(at, r1), :] = high
                    bl[pl.ds(at, r1), :] = low
            highs = jnp.concatenate([bh[pl.ds(at, r1), :] for at in spans[j]])
            lows = jnp.concatenate([bl[pl.ds(at, r1), :] for at in spans[j]])
            col = slice(h * wide, (h + 1) * wide)
            value = dot3(highs, lows, vh[:, col], vl[:, col]) * inv_cols
            for i in range(2):
                q = 2 * h + i
                for l, at in enumerate(spans[j]):
                    part[q, pl.ds(at, r1), :] = value[l * r1:(l + 1) * r1, i * 128:(i + 1) * 128]
                if h == 0 and j == 0 and i == 0:
                    pl.semaphore_wait(barrier, len(peers))
                for one in first[q]:
                    if j == 0:
                        one.relay()
                    if j == 2:
                        one.direct()
            if h == 1 and j == 2:
                add(0)
                add(1)

    def step1(q):
        for one, two in zip(first[q], second[q]):
            one.chunk(one.g.me)[...] = one.finish()
            two.start()

    def step2(q):
        for two, three in zip(second[q], third[q]):
            three.chunk(three.g.me)[...] = two.finish()
            three.start()

    def step3(q):
        for three, four in zip(third[q], fourth[q]):
            three.finish()
            four.start()

    def step4(q):
        pass

    add(2)
    add(3)
    for stage in (step1, step2, step3, step4):
        for q in range(4):
            stage(q)

    g0 = SumOver8(links, rz, core, partner, gram0, gpair0, gland0, gsum0)
    g1 = SumOver8(links, rz, core, partner, gram1, gpair1, gland1, gsum1)
    ws = [
        SumOver8(links, rz, core, partner, w.at[h], wpair.at[h], wland.at[h], wsum.at[h], True, h == 0) for h in range(2)
    ]

    def turned(q):
        step = 256
        for four in fourth[q]:
            four.finish()
        col = slice(q * 128, (q + 1) * 128)

        def body(i, c):
            at = pl.multiple_of(i * step, step)
            value = proj[q, pl.ds(at, step), :]
            ph[pl.ds(at, step), col], pl_[pl.ds(at, step), col] = split(value)
            pth[col, pl.ds(at, step)], ptl[col, pl.ds(at, step)] = split(value.T)
            return c + jnp.sum((value * value).reshape(step // 8, 8, 128), axis=0)

        return lax.fori_loop(0, rows // step, body, jnp.zeros((8, 128), F32))

    def products(h, i):
        at = h * wide + i * 128
        col = slice(at, at + 128)
        w[h, i * 128:(i + 1) * 128, :] = dot3(pth[col, :], ptl[col, :], bh[...], bl[...])

    squares = turned(0)
    squares = squares + turned(1)
    gram0[...] = dot3(pth[:wide, :], ptl[:wide, :], ph[:, :wide], pl_[:, :wide])
    g0.exchange()
    products(0, 0)
    g0.begin()
    products(0, 1)
    ws[0].exchange()
    squares = squares + turned(2)
    ws[0].begin()
    squares = squares + turned(3)
    tbuf[0] = squares
    tslots = [links.slot() for _ in range(4)]
    links.send(tslots[0], tbuf.at[0], tland.at[4], partner)
    gram1[...] = dot3(pth[wide:, :], ptl[wide:, :], ph[...], pl_[...])
    g1.exchange()
    links.landed(tslots[0], tland.at[4], partner)
    tland[z] = tbuf[0] + tland[4]
    for j in range(3):
        links.send(tslots[1 + j], tland.at[z], tland.at[z], rz.devices[j])
    g0.turn()
    products(1, 0)
    g1.begin()
    products(1, 1)
    ws[1].exchange()
    ws[0].mid()
    ws[1].begin()
    g0.forward()
    for j in range(3):
        links.landed(tslots[1 + j], tland.at[rz.sources[j]], rz.devices[j])
    shift = 0.0001 * jnp.sum(((tland[0] + tland[1]) + tland[2]) + tland[3]) / rank
    g0.end()

    rid = lax.broadcasted_iota(jnp.int32, (wide, wide), 0)
    cid = lax.broadcasted_iota(jnp.int32, (wide, wide), 1)
    diagonal = jnp.where(rid == cid, shift, 0.0)
    events = [None, g1.turn, ws[0].turn, None, ws[1].mid, None, g1.forward, g1.end,
              ws[0].forward, ws[1].turn, None, None, ws[0].last, None, None, ws[0].end]

    def event():
        e = events.pop(0)
        if e is not None:
            e()

    s0[...] = gsum0[...] + diagonal
    for k in range(wide // 128):
        factor_step(k, s0, a_ref, d_ref, r_ref, t_ref, event)
    inv0 = jnp.where(cid <= rid, s0[...], 0.0)
    s0[...] = inv0
    low = full(gsum1[:, :wide], inv0, NT)
    s1[...] = gsum1[:, wide:] + diagonal - full(low, low, NT)
    s2[...] = full(low, inv0)
    for k in range(wide // 128):
        factor_step(k, s1, a_ref, d_ref, r_ref, t_ref, event)
    inv1 = jnp.where(cid <= rid, s1[...], 0.0)
    x0h, x0l = split(s0[...])
    x1h, x1l = split(inv1)
    xch, xcl = split(-full(inv1, s2[...]))

    w0h, w0l = split(wsum[0])
    sums = []
    for h in range(2):
        col = slice(h * wide, (h + 1) * wide)
        if h == 0:
            back_t = dot3(x0h, x0l, w0h, w0l)
        else:
            ws[1].forward()
            ws[1].end()
            w1h, w1l = split(wsum[1])
            back_t = dot3(xch, xcl, w0h, w0l) + dot3(x1h, x1l, w1h, w1l)
        bth_ref[col, :], btl_ref[col, :] = split(back_t)
        back = back_t.T
        basis_ref[:, col] = back
        sums.append(jnp.sum(back * back, axis=0, keepdims=True))
    total = jnp.concatenate(sums, axis=1)
    colsum[...] = jnp.broadcast_to(total, colsum.shape)
    cslots = [links.slot() for _ in plane]
    for o, device in enumerate(plane):
        links.send(cslots[o], colsum, cland.at[o], device)
    outs = [(bth_ref, bth_hbm), (btl_ref, btl_hbm), (basis_ref, basis_hbm)]
    copies = []

    def store(src, dst):
        copies.append(pltpu.make_async_copy(src, dst, out_sem.at[len(copies)]))
        copies[-1].start()

    for src, dst in outs:
        store(src, dst)
    oh_ref[:, :wide], ol_ref[:, :wide] = split(dot3(ph[:, :wide], pl_[:, :wide], x0h, x0l, NT))
    oh_ref[:, wide:], ol_ref[:, wide:] = split(
        dot3(ph[:, :wide], pl_[:, :wide], xch, xcl, NT) + dot3(ph[:, wide:], pl_[:, wide:], x1h, x1l, NT)
    )
    store(oh_ref, oh_hbm)
    store(ol_ref, ol_hbm)
    for i in range(4):
        at = slice(i * rows // 4, (i + 1) * rows // 4)
        low = jnp.dot(oh_ref[at, :], bth_ref[...], preferred_element_type=F32)
        m_ref[at, :] = m_ref[at, :] + g_ref[at, :].astype(F32) - 0.05 * low
        store(m_ref.at[at, :], mo_hbm.at[at, :])
    links.drain()
    for o, device in enumerate(plane):
        links.landed(cslots[o], cland.at[o], device)
        total = total + cland[o, 0:1, :]
    sc_ref[...] = jnp.broadcast_to(1.0 / jnp.sqrt(total / COLS + 1e-06), sc_ref.shape)
    store(sc_ref, sc_hbm)
    for c in copies:
        c.wait()


def kernel_outputs(mi_ref, oh_ref, ol_ref, bth_ref, btl_ref, b_ref, sc_ref, mo_ref, bo_ref, u_ref):
    scale = sc_ref[0:1, :]
    ortho = oh_ref[...].astype(F32) + ol_ref[...].astype(F32)
    high, rest = split(ortho * (scale * jnp.sqrt(jnp.float32(ROWS) / RANK)))
    mo_ref[...] = mi_ref[...]
    u_ref[...] = dot3(high, rest, bth_ref[...], btl_ref[...]).astype(BF16)
    bo_ref[...] = b_ref[...] * scale


def sums_call(momentum, gradient, basis):
    rows, cols = momentum.shape
    rank = basis.shape[1]
    r1, r2, wide = rows // 8, rows // 32, rank // 2

    def mem(shape, kind=F32):
        return pltpu.VMEM(shape, kind)

    def out(shape, kind=F32):
        return jax.ShapeDtypeStruct(shape, kind)

    outs = (
        ((rows, rank), BF16), ((rows, rank), BF16), ((rank, cols), BF16), ((rank, cols), BF16),
        ((cols, rank), F32), ((8, rank), F32),
    )
    result = out((rows, cols))
    n = wide // 8
    anywhere = pl.BlockSpec(memory_space=pl.ANY)
    return pl.pallas_call(
        kernel_sums,
        out_shape=tuple(out(*o) for o in outs) + (result,),
        in_specs=[anywhere] * 3,
        out_specs=(anywhere,) * 7,
        scratch_shapes=[
            mem((rows, cols)), mem((rows, cols), BF16), mem((cols, rank)),
            *(mem(*o) for o in outs),
            mem((rows, cols), BF16), mem((rows, cols), BF16), mem((cols, rank), BF16), mem((cols, rank), BF16),
            mem((4, rows, 128)), mem((4, rows, 128)),
            mem((rows, rank), BF16), mem((rows, rank), BF16), mem((rank, rows), BF16), mem((rank, rows), BF16),
            mem((wide, wide)), mem((wide // 2, wide)), mem((3, n, wide)), mem((wide, wide)),
            mem((wide, rank)), mem((wide // 2, rank)), mem((3, n, rank)), mem((wide, rank)),
            mem((2, wide, cols)), mem((2, wide // 2, cols)), mem((2, 6, n // 2, cols)), mem((2, wide, cols)),
            mem((wide, wide)), mem((wide, wide)), mem((wide, wide)),
            mem((136, 128)), mem((128, 128)), mem((8, 128)), mem((136, 8)),
            mem((4, 6, r1 // 2, 128)), mem((4, 6, r1 // 2, 128)), mem((4, 3, r2, 128)), mem((4, 3, r2, 128)),
            mem((1, 8, 128)), mem((5, 8, 128)), mem((8, rank)), mem((15, 8, rank)),
            pltpu.SemaphoreType.DMA((17,)), pltpu.SemaphoreType.DMA((10,)),
            pltpu.SemaphoreType.DMA((208,)), pltpu.SemaphoreType.DMA((208,)),
        ],
        compiler_params=pltpu.CompilerParams(
            collective_id=0, has_side_effects=True, vmem_limit_bytes=62 * 2**20
        ),
        cost_estimate=pl.CostEstimate(flops=10 * 10**9, bytes_accessed=20 * 2**20, transcendentals=0),
    )(momentum, gradient, basis)


def shards(momentum, gradient, basis):
    rows, cols = momentum.shape
    rank = basis.shape[1]

    def out(shape, kind=F32):
        return jax.ShapeDtypeStruct(shape, kind)

    oh, ol, bth, btl, back, scale, corrected = sums_call(momentum, gradient, basis)
    tiles = 2
    tr, tc = rows // tiles, cols // tiles

    def rowed(width):
        return pl.BlockSpec((tr, width), lambda i: (i, 0))

    fixed = pl.BlockSpec((rank, cols), lambda i: (0, 0))
    cut_cols = pl.BlockSpec((tc, rank), lambda i: (i, 0))
    small = pl.BlockSpec((8, rank), lambda i: (0, 0))
    return pl.pallas_call(
        kernel_outputs,
        grid=(tiles,),
        out_shape=(out((rows, cols)), out((cols, rank)), out((rows, cols), BF16)),
        in_specs=[rowed(cols), rowed(rank), rowed(rank), fixed, fixed, cut_cols, small],
        out_specs=(rowed(cols), cut_cols, rowed(cols)),
        compiler_params=pltpu.CompilerParams(vmem_limit_bytes=62 * 2**20),
        cost_estimate=pl.CostEstimate(flops=4 * 10**9, bytes_accessed=18 * 2**20, transcendentals=0),
    )(corrected, oh, ol, bth, btl, back, scale)


def solution(mesh):
    placed = (P("fsdp", "tp"), P("fsdp", "tp"), P("tp", None))
    return jax.shard_map(
        shards,
        mesh=mesh,
        in_specs=placed,
        out_specs=(P("fsdp", "tp"), P("tp", None), P("fsdp", "tp")),
        check_vma=False,
    )
```
